256 devices in a mesh: expert: 16 (over z, core), edata: 4 (over x), tensor: 4 (over y).
Axes of the slice: x: 4, y: 4, z: 8, core: 2. Of those that a mesh axis runs over, the one named last changes fastest.
Arguments:
- out_grad: bfloat16 [4096, 3072], P(('expert', 'edata')), may hold values from -6 to 6
- router_probs: bfloat16 [4096, 4], P(('expert', 'edata')), may hold values from 0.049804688 to 0.5
- expert_ids: int32 [4096, 4], P(('expert', 'edata')), may hold values from 0 to 15, all different within a row; in each aligned block of 64 rows (0 to 63, 64 to 127, ...) at most 24 rows name the same one
- saved_gate: bfloat16 [16, 4, 16, 24, 5632], P('expert', 'edata', None, None, 'tensor'), may hold values from -6 to 6
- saved_up: bfloat16 [16, 4, 16, 24, 5632], P('expert', 'edata', None, None, 'tensor'), may hold values from -28 to 28
- down_weight: bfloat16 [16, 3072, 5632], P('expert', 'edata', 'tensor'), may hold values from -0.078125 to 0.078125
Outputs:
- gate_grad: bfloat16 [16, 4, 16, 24, 5632], P('expert', 'edata', None, None, 'tensor')
- up_grad: bfloat16 [16, 4, 16, 24, 5632], P('expert', 'edata', None, None, 'tensor')
- weight_grad: bfloat16 [16, 3072, 5632], P('expert', 'edata', 'tensor')
- router_grad: float32 [4096, 4], P(('expert', 'edata'))
The draws below stay inside these ranges and needn't reach their ends.
Inputs may be any that keep to these rules, and one draw needn't show every extreme that they name: `expert_ids`: each token names 4 different experts; among the 64 tokens of one shard no expert is named more than 24 times, and in some shards one is named exactly 24 times.
All inputs are finite; a program needn't handle non-finite values. Where the reference program divides by a largest or mean magnitude, that divisor is 1e-20 or more.
Results may differ from the reference program's by a relative error of at most 0.012.
Values may be sent and summed in bfloat16 or wider, within the bound.
A program may use at most 128 MiB of HBM per device.

```python
import math
import jax
import jax.numpy as jnp
import numpy as np
from jax import lax

D = 3072
FF = 5632
TOK_DEV = 64
EXPERTS = 16
TOP = 4
CAP = 24
SOURCES = 16
REPLICAS = 4
TOKENS = 4096


def draw_saved_up(key, part):
    key = jax.random.fold_in(key, 11)
    base_key, scale_key = jax.random.split(key)
    shape = (EXPERTS, REPLICAS, SOURCES, CAP, FF)
    rows_scale = jnp.exp(jax.random.uniform(scale_key, (EXPERTS, REPLICAS, SOURCES, CAP, 1), jnp.float32) * math.log(4.0))
    replica_place = (jnp.arange(REPLICAS, dtype=jnp.float32) / max(REPLICAS - 1, 1)).reshape(1, REPLICAS, 1, 1, 1)
    hidden_place = (jnp.arange(FF, dtype=jnp.float32) / FF).reshape(1, 1, 1, 1, FF)
    ramp_place = replica_place + hidden_place
    base_value = jnp.clip(jax.random.normal(base_key, shape, jnp.float32), -4.0, 4.0)
    ramp_value = jnp.exp(ramp_place * math.log(3.0))
    return (0.05 * base_value * rows_scale * ramp_value).astype(jnp.bfloat16)


def block_scale(stream_key, extent, shards, smallest, largest):
    def one(dim, parts):
        steps = jax.random.uniform(jax.random.fold_in(jax.random.fold_in(stream_key, 6), dim), (parts,), jnp.float32, smallest / len(shards), largest / len(shards))
        return jnp.repeat(jnp.exp(steps), extent[dim] // parts).reshape((-1,) + (1,) * (len(extent) - dim - 1))

    gain = one(*shards[0])
    for cut in shards[1:]:
        gain = gain * one(*cut)
    return gain


def shared_out(stream_key, own, number, rows, count, top, limit, skew):
    ranking = jax.random.permutation(stream_key, count)
    heavy_load, usual = load_shares(count, rows * top, limit, skew, True), load_shares(count, rows * top, limit, skew, False)
    places = jnp.arange(count)

    def named(sizes, offset_by):
        used = int((sizes > 0).sum())
        fixed = max(1, used // 4)
        shifted = fixed + (places - fixed + offset_by * (used - fixed)) % max(1, count - fixed)
        return jnp.zeros((count,), jnp.int32).at[ranking[jnp.where(places < fixed, places, shifted)]].set(jnp.asarray(sizes, jnp.int32))

    sizes = jnp.where(number % 4 == 0, named(heavy_load, number // 4), named(usual, number - number // 4 - 1))
    mixed = jax.random.permutation(jax.random.fold_in(own, 3), count)
    donor, sink = mixed[0:count // 2 * 2:2], mixed[1:count // 2 * 2:2]
    slack = jnp.minimum(sizes[donor] - 1, limit - sizes[sink]) // 2
    slack = jnp.where((donor == ranking[0]) | (sink == ranking[0]) | (sizes[sink] == 0), 0, jnp.maximum(slack, 0))
    shifted = jax.random.randint(jax.random.fold_in(own, 4), (count // 2,), 0, 1 << 20) % (slack + 1)
    sizes = sizes.at[donor].add(-shifted).at[sink].add(shifted)
    labels = jnp.searchsorted(jnp.cumsum(sizes), jnp.arange(rows * top), side="right").astype(jnp.int32)
    listing = labels.reshape(top, rows).T
    listing = listing[jax.random.permutation(jax.random.fold_in(own, 1), rows)]
    offset_by = jax.random.randint(jax.random.fold_in(own, 2), (rows, 1), 0, top)
    return jnp.take_along_axis(listing, (jnp.arange(top)[None, :] + offset_by) % top, axis=1)


def load_shares(amount, total, reach, lean, full):
    portions = [(1 << 20) // math.isqrt(rank ** lean) + 1 for rank in range(1, amount + 1)]
    largest = reach if full else min(reach, max(-(-total // amount), total * portions[0] // sum(portions)))
    least = 1 if total - largest >= amount - 1 else 0
    counts, surplus = [largest] + [least] * (amount - 1), total - largest - least * (amount - 1)
    while surplus > 0:
        candidates = [i for i in range(1, amount) if counts[i] < largest] or [i for i in range(1, amount) if counts[i] < reach]
        whole, remaining = sum([portions[i] for i in candidates]), surplus
        for i in candidates:
            more = min(reach - counts[i], max(1, remaining * portions[i] // whole), surplus)
            counts[i] = counts[i] + more
            surplus = surplus - more
    return np.array(counts)


def normal_values(own_key, dims, deviation, bound, shards=(), kind=jnp.bfloat16):
    gain = block_scale(own_key, dims, shards, -0.22, 0.18) if shards else 1.0
    values = jax.random.normal(own_key, dims, jnp.float32) * deviation * gain
    return jnp.minimum(jnp.maximum(values, -bound), bound).astype(kind)


def setup_inputs(seed: int = 0) -> dict:
    arg_keys = jax.random.split(jax.random.key(seed), 7)
    out_grad = normal_values(arg_keys[0], (TOKENS, D), 1.0, 6.0, ((0, 64),))
    router_probs = jnp.clip(0.049804688 + 0.4501953 * jax.random.uniform(arg_keys[1], (TOKENS, TOP), jnp.float32) ** block_scale(arg_keys[1], (TOKENS, TOP), ((0, 64),), -0.2, 0.2), 0.049804688, 0.5).astype(jnp.bfloat16)
    expert_ids_keys = jax.random.split(jax.random.fold_in(arg_keys[2], 1), TOKENS // TOK_DEV)
    expert_ids_turns = jax.random.permutation(jax.random.fold_in(arg_keys[2], 3), TOKENS // TOK_DEV)
    expert_ids = jax.vmap(lambda own, number: shared_out(jax.random.fold_in(arg_keys[2], 2), own, number, TOK_DEV, EXPERTS, TOP, CAP, 2))(expert_ids_keys, expert_ids_turns).reshape((TOKENS, TOP))
    saved_gate = normal_values(arg_keys[3], (EXPERTS, REPLICAS, SOURCES, CAP, FF), 1.0, 6.0, ((0, 16), (1, 4), (4, 4)))
    saved_up = draw_saved_up(jax.random.fold_in(arg_keys[6], 71), 0)
    down_weight = normal_values(arg_keys[5], (EXPERTS, D, FF), FF ** -0.5, 0.078125, ((0, 16), (1, 4), (2, 4)))
    return dict(out_grad=out_grad, router_probs=router_probs, expert_ids=expert_ids, saved_gate=saved_gate, saved_up=saved_up, down_weight=down_weight)


def slot_numbers(expert_ids):
    blocks = expert_ids.reshape(-1, TOK_DEV * TOP)
    matches = (blocks[:, :, None] == jnp.arange(EXPERTS, dtype=jnp.int32)[None, None, :]).astype(jnp.int32)
    earlier = jnp.cumsum(matches, axis=1) - matches
    return jnp.sum(earlier * matches, axis=2).reshape(-1).astype(jnp.int32)


def silu_backward(d_hidden, gate_value, up_value):
    sigmoid_gate = jax.nn.sigmoid(gate_value)
    activated = gate_value * sigmoid_gate
    gate_delta = d_hidden * up_value * sigmoid_gate * (1.0 + gate_value * (1.0 - sigmoid_gate))
    up_delta = d_hidden * activated
    return activated * up_value, gate_delta, up_delta


def reference(out_grad, router_probs, expert_ids, saved_gate, saved_up, down_weight):
    slot_index = slot_numbers(expert_ids)
    pair_index = jnp.arange(TOKENS * TOP, dtype=jnp.int32)
    token_index = pair_index // TOP
    source_index = token_index // (REPLICAS * TOK_DEV)
    replica_index = (token_index // TOK_DEV) % REPLICAS
    flat_ids = expert_ids.reshape(-1).astype(jnp.int32)
    position = (((flat_ids * REPLICAS + replica_index) * SOURCES + source_index) * CAP + slot_index).astype(jnp.int32)
    owner_pair = jnp.full((EXPERTS * REPLICAS * SOURCES * CAP,), -1, jnp.int32).at[position].set(pair_index)
    filled = owner_pair >= 0
    owner_safe = jnp.where(filled, owner_pair, 0).astype(jnp.int32)
    slot_probs = jnp.where(filled, router_probs.reshape(-1)[owner_safe], jnp.zeros((), router_probs.dtype))
    slot_probs = slot_probs.reshape(EXPERTS, -1)
    slot_tokens = (owner_safe // TOP).astype(jnp.int32).reshape(EXPERTS, -1)
    slot_filled = filled.reshape(EXPERTS, -1)

    def per_expert(inputs):
        tokens_here, filled_here, probs_here, gate_here, up_here, weight_here = inputs
        routed = jnp.where(filled_here[:, None], out_grad[tokens_here], jnp.zeros((), out_grad.dtype))
        back_grad = jnp.dot(routed, weight_here, preferred_element_type=jnp.float32)
        gate_value = gate_here.reshape(-1, FF).astype(jnp.float32)
        up_value = up_here.reshape(-1, FF).astype(jnp.float32)
        probs_float = probs_here.astype(jnp.float32)[:, None]
        hidden, gate_delta, up_delta = silu_backward(probs_float * back_grad, gate_value, up_value)
        router_slot = jnp.sum(hidden * back_grad, axis=1)
        gate_peak = jnp.max(jnp.abs(gate_delta))
        up_peak = jnp.max(jnp.abs(up_delta))
        gate_out = (gate_delta / (gate_peak + 1e-6)).astype(jnp.bfloat16)
        up_out = (up_delta / (up_peak + 1e-6)).astype(jnp.bfloat16)
        scaled_rows = (routed.astype(jnp.float32) * probs_float).astype(jnp.bfloat16)
        hidden_rounded = hidden.astype(jnp.bfloat16)
        weight_sum = lax.dot_general(scaled_rows, hidden_rounded, (((0,), (0,)), ((), ())), preferred_element_type=jnp.float32)
        return gate_out, up_out, weight_sum.astype(jnp.bfloat16), router_slot

    gate_all, up_all, weight_grad, router_slots = lax.map(per_expert, (slot_tokens, slot_filled, slot_probs, saved_gate, saved_up, down_weight))
    gate_grad = gate_all.reshape(EXPERTS, REPLICAS, SOURCES, CAP, FF)
    up_grad = up_all.reshape(EXPERTS, REPLICAS, SOURCES, CAP, FF)
    router_grad = router_slots.reshape(-1)[position].reshape(TOKENS, TOP)
    return gate_grad, up_grad, weight_grad, router_grad
```

```python
import functools

import jax
import jax.numpy as jnp
from jax import lax
from jax.experimental import pallas as pl
from jax.experimental.pallas import tpu as pltpu
from jax.sharding import PartitionSpec as P

MESH = pl.DeviceIdType.MESH
RING = 4
F32 = jnp.float32
BF16 = jnp.bfloat16


def local(src, dst, sem):
    return pltpu.make_async_copy(src, dst, sem)


def silu_factors(gate_value, up_value):
    sigmoid_gate = jax.nn.sigmoid(gate_value)
    activated = gate_value * sigmoid_gate
    gate_factor = up_value * sigmoid_gate * (1.0 + gate_value * (1.0 - sigmoid_gate))
    return activated * up_value, gate_factor, activated


def kernel(
    experts, cap, tok, top,
    og, ids_ref, probs_ref, gate, up, w,
    gate_out, up_out, wg_out, router_out,
    gate_v, up_v, w_v, a_gate, a_up, hid, rows, x2, meta_own, meta_in, target_v, scale_v, sb,
    sb_o, sb_d, sb_c, rb_o, rb_d, rb_c, keep, own, wg_v, g_v, u_v,
    pk_own, pk_in, rl, rz_out, rz_in, ry_own, ry_in,
    load_sem, xs, xr, ms, mr, zs, zr, ys, yr_, hs, hr, bs, br, ps, pr, ws, wr, vs, vr, out_sem,
):
    e, x, y = lax.axis_index("expert"), lax.axis_index("edata"), lax.axis_index("tensor")
    z, c = lax.div(e, 2), lax.rem(e, 2)
    slots, width = gate.shape
    half = slots // 2
    quarter = half // 2
    features = w.shape[0]
    lanes_half = features // 2
    pair = 2 * cap
    x_right, x_left, x_far = lax.rem(x + 1, RING), lax.rem(x + 3, RING), lax.rem(x + 2, RING)
    y_right, y_left, y_far = lax.rem(y + 1, RING), lax.rem(y + 3, RING), lax.rem(y + 2, RING)
    first, second = pl.ds(0, half), pl.ds(half, half)

    loads = []
    for i, part in enumerate((first, second)):
        loads.append((
            local(gate.at[part], gate_v.at[part], load_sem.at[2 * i]),
            local(up.at[part], up_v.at[part], load_sem.at[2 * i + 1]),
        ))
    load_w = local(w, w_v, load_sem.at[4])
    for pair_of in loads:
        for copy in pair_of:
            copy.start()
    load_w.start()

    barrier = pltpu.get_barrier_semaphore()

    def greet(device):
        pl.semaphore_signal(barrier, inc=1, device_id=device, device_id_type=MESH)

    @pl.loop(1, experts)
    def _(i):
        greet((lax.rem(e + i, experts), x, y))

    @pl.loop(1, RING * RING)
    def _(i):
        p = lax.rem(x * RING + y + i, RING * RING)
        greet((e, lax.div(p, RING), lax.rem(p, RING)))

    @pl.when(x != y)
    def _():
        greet((2 * z + 1 - c, y, x))

    place = (
        lax.broadcasted_iota(jnp.int32, (tok, 128), 1)
        == lax.broadcasted_iota(jnp.int32, (tok, 128), 0) + tok * c
    ).astype(F32).astype(BF16)
    meta_own[0:top, :] = jnp.dot(
        ids_ref[...].astype(F32).astype(BF16), place, preferred_element_type=F32
    )
    meta_own[4:4 + top, :] = jnp.dot(probs_ref[...], place, preferred_element_type=F32)

    peers = experts - 1 + RING * RING - 1
    pl.semaphore_wait(barrier, jnp.where(x == y, peers, peers + 1))

    def swap(core):
        lanes = pl.ds(pl.multiple_of(features * y + lanes_half * core, 128), lanes_half)
        device = (2 * z + core, y, x)
        return (
            pltpu.make_async_remote_copy(
                src_ref=meta_own, dst_ref=meta_in.at[c], send_sem=ms.at[core],
                recv_sem=mr.at[c], device_id=device, device_id_type=MESH,
            ),
            pltpu.make_async_remote_copy(
                src_ref=og.at[:, lanes], dst_ref=x2.at[c], send_sem=xs.at[core],
                recv_sem=xr.at[c], device_id=device, device_id_type=MESH,
            ),
        )

    for core in range(2):
        at_home = jnp.logical_and(x == y, c == core)

        @pl.when(at_home)
        def _():
            lanes = pl.ds(pl.multiple_of(features * y + lanes_half * core, 128), lanes_half)
            local(meta_own, meta_in.at[c], mr.at[c]).start()
            local(og.at[:, lanes], x2.at[c], xr.at[c]).start()

        @pl.when(jnp.logical_not(at_home))
        def _():
            for copy in swap(core):
                copy.start()

    def ring_copy(buf, block, part, axis, to_right, send, recv, index):
        if axis == "edata":
            device = (e, x_right if to_right else x_left, y)
        else:
            device = (e, x, y_right if to_right else y_left)
        return pltpu.make_async_remote_copy(
            src_ref=buf.at[block, part], dst_ref=buf.at[block, part],
            send_sem=send.at[index], recv_sem=recv.at[index],
            device_id=device, device_id_type=MESH,
        )

    def ring(buf, me, left, right, axis, send, recv):
        make = functools.partial(ring_copy, buf, axis=axis, send=send, recv=recv)
        return dict(
            r0=make(block=me, part=first, to_right=True, index=0),
            r1=make(block=me, part=second, to_right=True, index=1),
            l0=make(block=me, part=first, to_right=False, index=2),
            l1=make(block=me, part=second, to_right=False, index=3),
            rf=make(block=left, part=first, to_right=True, index=4),
            lf=make(block=right, part=second, to_right=False, index=5),
        )

    h_ring = ring(hid, x, x_left, x_right, "edata", hs, hr)
    y_ring = ring(rows, y, y_left, y_right, "tensor", ys, yr_)

    def hidden_of(base):
        @pl.loop(0, half // 16)
        def _(i):
            part = pl.ds(pl.multiple_of(base + i * 16, 16), 16)
            hidden, gate_factor, up_factor = silu_factors(
                gate_v[part, :].astype(F32), up_v[part, :].astype(F32)
            )
            hid[x, part, :] = hidden.astype(BF16)
            a_gate[part, :] = gate_factor
            a_up[part, :] = up_factor

    for copy in loads[0]:
        copy.wait()
    hidden_of(0)
    h_ring["r0"].start()
    for copy in loads[1]:
        copy.wait()
    hidden_of(half)
    h_ring["l1"].start()
    h_ring["r1"].start()
    h_ring["l0"].start()

    for core in range(2):
        local(meta_own, meta_in.at[core], mr.at[core]).wait()
        local(x2.at[core], x2.at[core], xr.at[core]).wait()
    meta = meta_in[0] + meta_in[1]
    lane = lax.broadcasted_iota(jnp.int32, (experts, 128), 1)
    expert_row = lax.broadcasted_iota(jnp.int32, (experts, 128), 0).astype(F32)
    member = jnp.zeros((experts, 128), F32)
    scale = jnp.zeros((experts, 128), F32)
    for k in range(top):
        named = meta[k:k + 1, :] == expert_row
        member = jnp.where(named, 1.0, member)
        scale = jnp.where(named, meta[4 + k:5 + k, :], scale)
    live = lane < 2 * tok
    member = jnp.where(live, member, 0.0)
    row_i = lax.broadcasted_iota(jnp.int32, (128, 128), 0)
    lane_i = lax.broadcasted_iota(jnp.int32, (128, 128), 1)
    before = jnp.logical_and(row_i < lane_i, jnp.logical_or(row_i >= tok, lane_i < tok))
    earlier = jnp.dot(
        member.astype(BF16), before.astype(F32).astype(BF16), preferred_element_type=F32
    )
    target_v[...] = jnp.where(
        member > 0.0, earlier + jnp.where(lane >= tok, float(cap), 0.0), -1.0
    )
    scale_v[...] = scale
    slot_row = lax.broadcasted_iota(jnp.int32, (pair, 128), 0).astype(F32)
    my_rows = pl.ds(pl.multiple_of(pair * z, 16), pair)
    my_lanes = pl.ds(pl.multiple_of(lanes_half * c, 128), lanes_half)

    def dispatch(to):
        return pltpu.make_async_remote_copy(
            src_ref=sb.at[pl.ds(pl.multiple_of(pair * to, 16), pair)],
            dst_ref=rows.at[y, my_rows, my_lanes],
            send_sem=zs.at[to], recv_sem=zr.at[e],
            device_id=(to, x, y), device_id_type=MESH,
        )

    @pl.loop(0, experts)
    def _(i):
        to = lax.rem(e + i + 1, experts)
        pick = jnp.where(
            slot_row == target_v[pl.ds(to, 1), :], scale_v[pl.ds(to, 1), :], 0.0
        ).astype(BF16)
        tokens = x2[...].reshape(2 * tok, lanes_half)
        block = jnp.dot(pick[:, :2 * tok], tokens, preferred_element_type=F32)
        sb[pl.ds(pl.multiple_of(pair * to, 16), pair), :] = block.astype(BF16)

        @pl.when(to != e)
        def _():
            dispatch(to).start()

        @pl.when(to == e)
        def _():
            local(
                sb.at[pl.ds(pl.multiple_of(pair * to, 16), pair)],
                rows.at[y, my_rows, my_lanes], zr.at[e],
            ).start()

    def arrived(start):
        @pl.loop(start, start + experts // 2)
        def _(s):
            at = rows.at[
                y, pl.ds(pl.multiple_of(pair * lax.div(s, 2), 16), pair),
                pl.ds(pl.multiple_of(lanes_half * lax.rem(s, 2), 128), lanes_half),
            ]
            local(at, at, zr.at[s]).wait()

    arrived(0)
    y_ring["r0"].start()
    y_ring["l0"].start()
    arrived(experts // 2)
    y_ring["l1"].start()
    y_ring["r1"].start()

    h_ring["r0"].wait_recv()
    h_ring["rf"].start()
    h_ring["l1"].wait_recv()
    h_ring["lf"].start()
    y_ring["r0"].wait_recv()
    y_ring["rf"].start()
    y_ring["l1"].wait_recv()
    y_ring["lf"].start()
    load_w.wait()
    for name in ("r1", "l0", "rf", "lf"):
        y_ring[name].wait_recv()

    tiles = [(at, min(256, width - at)) for at in range(0, width, 256)]

    def partial(replica, store0, store1):
        block = rows[replica]
        for at, size in tiles:
            product = jnp.dot(block, w_v[:, at:at + size], preferred_element_type=F32)
            store0(at, size, product[:half])
            store1(at, size, product[half:])

    def keep_in(ref, kind):
        def store(at, size, value):
            ref[:, at:at + size] = value.astype(kind)
        return store

    def send(index, src, dst, to_right):
        return pltpu.make_async_remote_copy(
            src_ref=src, dst_ref=dst, send_sem=bs.at[index], recv_sem=br.at[index],
            device_id=(e, x_right if to_right else x_left, y), device_id_type=MESH,
        )

    part_a, part_b = pl.ds(0, quarter), pl.ds(quarter, quarter)
    far0 = send(0, sb_o.at[0], rb_o.at[0], True)
    far1 = send(1, sb_o.at[1], rb_o.at[1], False)
    near0 = send(2, sb_d.at[0], rb_d.at[0], True)
    near1 = send(3, sb_d.at[1], rb_d.at[1], False)
    both = [
        (send(4 + 2 * i, sb_c.at[0, part], rb_c.at[0, part], True),
         send(5 + 2 * i, sb_c.at[1, part], rb_c.at[1, part], False))
        for i, part in enumerate((part_a, part_b))
    ]
    partial(x_far, keep_in(sb_o.at[0], BF16), keep_in(sb_o.at[1], BF16))
    far0.start()
    far1.start()
    partial(x_right, keep_in(keep.at[0], F32), keep_in(sb_d.at[0], BF16))
    near0.start()
    partial(x_left, keep_in(sb_d.at[1], BF16), keep_in(keep.at[1], F32))
    near1.start()
    partial(x, keep_in(own.at[0], F32), keep_in(own.at[1], F32))

    for name in ("r1", "l0", "rf", "lf"):
        h_ring[name].wait_recv()
    all_hidden = hid[...].reshape(RING * slots, width)
    step = 256 if features % 256 == 0 else 128
    wg_copies = []
    for i in range(features // step):
        at = pl.ds(i * step, step)
        wg_v[at, :] = lax.dot_general(
            rows[:, :, i * step:(i + 1) * step].reshape(RING * slots, step), all_hidden,
            (((0,), (0,)), ((), ())), preferred_element_type=F32,
        ).astype(BF16)
        wg_copies.append(local(wg_v.at[at], wg_out.at[at], out_sem.at[i]))
        wg_copies[-1].start()

    far0.wait_recv()
    far1.wait_recv()
    for i, pair_of in enumerate(both):
        @pl.loop(0, quarter // 16)
        def _(j):
            part = pl.ds(pl.multiple_of(i * quarter + j * 16, 16), 16)
            for side in range(2):
                sb_c[side, part, :] = (
                    keep[side, part, :] + rb_o[side, part, :].astype(F32)
                ).astype(BF16)
        for copy in pair_of:
            copy.start()
    near0.wait_recv()
    near1.wait_recv()

    zero = jnp.zeros((16, 128), F32)
    peaks = (zero, zero)
    for i, pair_of in enumerate(both):
        for copy in pair_of:
            copy.wait_recv()
        for side in range(2):
            def body(j, carry):
                gate_peak, up_peak = carry
                part = pl.ds(pl.multiple_of(i * quarter + j * 16, 16), 16)
                at = pl.ds(pl.multiple_of(side * half + i * quarter + j * 16, 16), 16)
                sent = rb_d[1 - side, part, :].astype(F32) + rb_c[side, part, :].astype(F32)
                d_hidden = own[side, part, :] + sent
                gate_delta = d_hidden * a_gate[at, :]
                up_delta = d_hidden * a_up[at, :]
                a_gate[at, :] = gate_delta
                a_up[at, :] = up_delta
                weighted = up_delta * up_v[at, :].astype(F32)
                total = zero
                for lane0 in range(0, width, 128):
                    sl = slice(lane0, lane0 + 128)
                    gate_peak = jnp.maximum(gate_peak, jnp.abs(gate_delta[:, sl]))
                    up_peak = jnp.maximum(up_peak, jnp.abs(up_delta[:, sl]))
                    total = total + weighted[:, sl]
                rl[at, :] = total
                return gate_peak, up_peak

            peaks = lax.fori_loop(0, quarter // 16, body, peaks)
    for i in range(2):
        pk_own[i] = jnp.maximum(peaks[i][:8], peaks[i][8:])
    me = x * RING + y
    pk_in[me] = pk_own[...]

    def tell_peak(p):
        return pltpu.make_async_remote_copy(
            src_ref=pk_own, dst_ref=pk_in.at[me], send_sem=ps.at[p], recv_sem=pr.at[me],
            device_id=(e, lax.div(p, RING), lax.rem(p, RING)), device_id_type=MESH,
        )

    @pl.loop(1, RING * RING)
    def _(i):
        tell_peak(lax.rem(me + i, RING * RING)).start()

    rl[slots:, :] = jnp.zeros((rl.shape[0] - slots, 128), F32)
    ones = jnp.ones((8, 128), BF16)
    across = (((1,), (1,)), ((), ()))

    def give_back(to):
        return pltpu.make_async_remote_copy(
            src_ref=rz_out.at[to], dst_ref=rz_in.at[e], send_sem=ws.at[to], recv_sem=wr.at[e],
            device_id=(to, x, y), device_id_type=MESH,
        )

    @pl.loop(0, experts)
    def _(i):
        to = lax.rem(e + i, experts)
        seg = rl[pl.ds(pl.multiple_of(cap * to, 8), 128), :]
        high = seg.astype(BF16)
        low = (seg - high.astype(F32)).astype(BF16)
        rz_out[to] = lax.dot_general(
            ones, high, across, preferred_element_type=F32
        ) + lax.dot_general(ones, low, across, preferred_element_type=F32)

        @pl.when(to != e)
        def _():
            give_back(to).start()

    rz_in[e] = rz_out[e]

    @pl.loop(1, RING * RING)
    def _(i):
        p = lax.rem(me + i, RING * RING)
        local(pk_in.at[p], pk_in.at[p], pr.at[p]).wait()

    all_peaks = jnp.max(pk_in[...], axis=0)
    gate_scale = 1.0 / (jnp.max(all_peaks[0], axis=(0, 1), keepdims=True) + 1e-6)
    up_scale = 1.0 / (jnp.max(all_peaks[1], axis=(0, 1), keepdims=True) + 1e-6)

    def scaled(base):
        @pl.loop(0, half // 16)
        def _(j):
            part = pl.ds(pl.multiple_of(base + j * 16, 16), 16)
            g_v[part, :] = (a_gate[part, :] * gate_scale).astype(BF16)
            u_v[part, :] = (a_up[part, :] * up_scale).astype(BF16)

    outs = []
    for i, part in enumerate((first, second)):
        scaled(i * half)
        outs.append(local(g_v.at[part], gate_out.at[part], out_sem.at[8 + 2 * i]))
        outs.append(local(u_v.at[part], up_out.at[part], out_sem.at[9 + 2 * i]))
        outs[-1].start()
        outs[-2].start()

    @pl.loop(1, experts)
    def _(i):
        s = lax.rem(e + i, experts)
        local(rz_in.at[s], rz_in.at[s], wr.at[s]).wait()

    ry_own[...] = rz_in[:, 0, :]

    def tell_sum(p):
        return pltpu.make_async_remote_copy(
            src_ref=ry_own, dst_ref=ry_in.at[y], send_sem=vs.at[p], recv_sem=vr.at[y],
            device_id=(e, x, p), device_id_type=MESH,
        )

    for p in (y_right, y_left, y_far):
        tell_sum(p).start()
    ids_f = ids_ref[...].astype(F32)
    expert_col = lax.broadcasted_iota(jnp.int32, (experts, tok), 0).astype(F32)
    named = [(ids_f[k:k + 1, :] == expert_col).astype(F32) for k in range(top)]
    tri = (
        lax.broadcasted_iota(jnp.int32, (tok, tok), 0)
        < lax.broadcasted_iota(jnp.int32, (tok, tok), 1)
    ).astype(F32).astype(BF16)
    earlier = jnp.dot(sum(named).astype(BF16), tri, preferred_element_type=F32)
    slot_col = lax.broadcasted_iota(jnp.int32, (128, tok), 0).astype(F32)
    at_slot = [
        slot_col == jnp.sum(earlier * named[k], axis=0, keepdims=True) for k in range(top)
    ]
    for p in (y_right, y_left, y_far):
        local(ry_in.at[p], ry_in.at[p], vr.at[p]).wait()
    sums = ry_own[...]
    for p in (y_right, y_left, y_far):
        sums = sums + ry_in[p]
    high = sums.astype(BF16)
    low = (sums - high.astype(F32)).astype(BF16)
    down = (((0,), (0,)), ((), ()))
    for k in range(top):
        pick = named[k].astype(BF16)
        found = lax.dot_general(
            high, pick, down, preferred_element_type=F32
        ) + lax.dot_general(low, pick, down, preferred_element_type=F32)
        value = jnp.sum(jnp.where(at_slot[k], found, 0.0), axis=0, keepdims=True)
        router_out[k:k + 1, :] = value / probs_ref[k:k + 1, :].astype(F32)

    for copy in wg_copies + outs:
        copy.wait()
    for core in range(2):
        @pl.when(jnp.logical_not(jnp.logical_and(x == y, c == core)))
        def _():
            for copy in swap(core):
                copy.wait_send()

    @pl.loop(1, experts)
    def _(i):
        to = lax.rem(e + i, experts)
        dispatch(to).wait_send()
        give_back(to).wait_send()

    @pl.loop(1, RING * RING)
    def _(i):
        tell_peak(lax.rem(me + i, RING * RING)).wait_send()

    for p in (y_right, y_left, y_far):
        tell_sum(p).wait_send()
    for name in ("r0", "r1", "l0", "l1", "rf", "lf"):
        h_ring[name].wait_send()
        y_ring[name].wait_send()
    for copy in (far0, far1, near0, near1) + both[0] + both[1]:
        copy.wait_send()


def shards(out_grad, router_probs, expert_ids, saved_gate, saved_up, down_weight):
    tok, top = expert_ids.shape
    experts = lax.axis_size("expert")
    cap = saved_gate.shape[3]
    width = saved_gate.shape[4]
    slots = saved_gate.shape[2] * cap
    features = down_weight.shape[1]
    half = slots // 2
    any_space = pl.BlockSpec(memory_space=pl.ANY)
    vmem = pl.BlockSpec(memory_space=pltpu.VMEM)
    dma = pltpu.SemaphoreType.DMA
    gate_grad, up_grad, weight_grad, router_grad = pl.pallas_call(
        functools.partial(kernel, experts, cap, tok, top),
        out_shape=(
            jax.ShapeDtypeStruct((slots, width), BF16),
            jax.ShapeDtypeStruct((slots, width), BF16),
            jax.ShapeDtypeStruct((features, width), BF16),
            jax.ShapeDtypeStruct((top, tok), F32),
        ),
        in_specs=[any_space, vmem, vmem, any_space, any_space, any_space],
        out_specs=(any_space, any_space, any_space, vmem),
        scratch_shapes=[
            pltpu.VMEM((slots, width), BF16),
            pltpu.VMEM((slots, width), BF16),
            pltpu.VMEM((features, width), BF16),
            pltpu.VMEM((slots, width), F32),
            pltpu.VMEM((slots, width), F32),
            pltpu.VMEM((RING, slots, width), BF16),
            pltpu.VMEM((RING, slots, features), BF16),
            pltpu.VMEM((2, tok, features // 2), BF16),
            pltpu.VMEM((8, 128), F32),
            pltpu.VMEM((2, 8, 128), F32),
            pltpu.VMEM((experts, 128), F32),
            pltpu.VMEM((experts, 128), F32),
            pltpu.VMEM((2 * cap * experts, features // 2), BF16),
            pltpu.VMEM((2, half, width), BF16),
            pltpu.VMEM((2, half, width), BF16),
            pltpu.VMEM((2, half, width), BF16),
            pltpu.VMEM((2, half, width), BF16),
            pltpu.VMEM((2, half, width), BF16),
            pltpu.VMEM((2, half, width), BF16),
            pltpu.VMEM((2, half, width), F32),
            pltpu.VMEM((2, half, width), F32),
            pltpu.VMEM((features, width), BF16),
            pltpu.VMEM((slots, width), BF16),
            pltpu.VMEM((slots, width), BF16),
            pltpu.VMEM((2, 8, 128), F32),
            pltpu.VMEM((RING * RING, 2, 8, 128), F32),
            pltpu.VMEM((slots + 128, 128), F32),
            pltpu.VMEM((experts, 8, 128), F32),
            pltpu.VMEM((experts, 8, 128), F32),
            pltpu.VMEM((experts, 128), F32),
            pltpu.VMEM((RING, experts, 128), F32),
            dma((5,)),
            dma((2,)), dma((2,)), dma((2,)), dma((2,)),
            dma((experts,)), dma((experts,)),
            dma((6,)), dma((6,)), dma((6,)), dma((6,)),
            dma((8,)), dma((8,)),
            dma((RING * RING,)), dma((RING * RING,)),
            dma((experts,)), dma((experts,)),
            dma((RING,)), dma((RING,)),
            dma((12,)),
        ],
        compiler_params=pltpu.CompilerParams(
            collective_id=0, has_side_effects=True, vmem_limit_bytes=56 * 1024 * 1024
        ),
        cost_estimate=pl.CostEstimate(
            flops=4 * RING * slots * features * width,
            bytes_accessed=8 * slots * width + 4 * features * width,
            transcendentals=slots * width,
        ),
    )(
        out_grad, expert_ids.T, router_probs.T, saved_gate.reshape(slots, width),
        saved_up.reshape(slots, width), down_weight.reshape(features, width),
    )
    return (
        gate_grad.reshape(saved_gate.shape), up_grad.reshape(saved_up.shape),
        weight_grad.reshape(down_weight.shape), router_grad.T,
    )


def solution(mesh):
    in_specs = (
        P(("expert", "edata"), None),
        P(("expert", "edata"), None),
        P(("expert", "edata"), None),
        P("expert", "edata", None, None, "tensor"),
        P("expert", "edata", None, None, "tensor"),
        P("expert", "edata", "tensor"),
    )
    out_specs = (
        P("expert", "edata", None, None, "tensor"),
        P("expert", "edata", None, None, "tensor"),
        P("expert", "edata", "tensor"),
        P(("expert", "edata"), None),
    )
    return jax.shard_map(shards, mesh=mesh, in_specs=in_specs, out_specs=out_specs, check_vma=False)
```

```python
import functools

import jax
import jax.numpy as jnp
from jax import lax
from jax.experimental import pallas as pl
from jax.experimental.pallas import tpu as pltpu
from jax.sharding import PartitionSpec as P

MESH = pl.DeviceIdType.MESH
RING = 4
F32 = jnp.float32
BF16 = jnp.bfloat16


def local(src, dst, sem):
    return pltpu.make_async_copy(src, dst, sem)


def silu_factors(gate_value, up_value):
    sigmoid_gate = jax.nn.sigmoid(gate_value)
    activated = gate_value * sigmoid_gate
    gate_factor = up_value * sigmoid_gate * (1.0 + gate_value * (1.0 - sigmoid_gate))
    return activated * up_value, gate_factor, activated


def kernel(
    experts, cap, tok, top,
    og, ids, probs, gate, up, w,
    gate_out, up_out, wg_out, router_out,
    ids_ref, probs_ref, og_v, gate_v, up_v, w_v, a_gate, a_up, hid, rows, x2, meta_own, meta_in, sb,
    part_f, part_b, sb_c, rb_o, rb_d, rb_c, wg_acc,
    pk_own, pk_in, pk_row, pk_rows, rl, rz_out, rz_in, ry_own, ry_in,
    load_sem, xs, xr, ms, mr, zs, zr, ys, yr, hs, hr, bs, br, ps, pr, qs, qr, ws, wr, vs, vr,
):
    e, x, y = lax.axis_index("expert"), lax.axis_index("edata"), lax.axis_index("tensor")
    z, c = lax.div(e, 2), lax.rem(e, 2)
    slots, width = gate.shape
    half = slots // 2
    quarter = half // 2
    features = w.shape[0]
    lanes_half = features // 2
    pair = 2 * cap
    x_right, x_left, x_far = lax.rem(x + 1, RING), lax.rem(x + 3, RING), lax.rem(x + 2, RING)
    y_right, y_left, y_far = lax.rem(y + 1, RING), lax.rem(y + 3, RING), lax.rem(y + 2, RING)
    first, second = pl.ds(0, half), pl.ds(half, half)

    def share(core):
        return lax.rem(y - x + 2 * core + RING, RING)

    from_y = lax.rem(x + y + 2 * c, RING)
    gives_home = jnp.logical_and(share(1 - c) == x, x == y)
    takes_home = jnp.logical_and(from_y == y, x == y)
    stays = jnp.logical_and(share(c) == x, x == y)

    loads = []
    for i, part in enumerate((first, second)):
        loads.append((
            local(gate.at[part], gate_v.at[part], load_sem.at[2 * i]),
            local(up.at[part], up_v.at[part], load_sem.at[2 * i + 1]),
        ))
    load_w = local(w, w_v, load_sem.at[4])
    small = (
        local(ids, ids_ref, load_sem.at[5]),
        local(probs, probs_ref, load_sem.at[6]),
    ) + tuple(
        local(
            og.at[:, pl.ds(
                pl.multiple_of(features * share(core) + lanes_half * core, 128), lanes_half
            )],
            og_v.at[core], load_sem.at[7 + core],
        )
        for core in range(2)
    )
    for copy in small:
        copy.start()
    for pair_of in loads:
        for copy in pair_of:
            copy.start()
    load_w.start()

    barrier = pltpu.get_barrier_semaphore()

    def greet(device):
        pl.semaphore_signal(barrier, inc=1, device_id=device, device_id_type=MESH)

    @pl.loop(1, experts)
    def _(i):
        greet((lax.rem(e + i, experts), x, y))

    @pl.loop(1, RING * RING)
    def _(i):
        p = lax.rem(x * RING + y + i, RING * RING)
        greet((e, lax.div(p, RING), lax.rem(p, RING)))

    @pl.when(jnp.logical_not(gives_home))
    def _():
        greet((2 * z + 1 - c, share(1 - c), x))

    @pl.when(jnp.logical_not(takes_home))
    def _():
        greet((2 * z + 1 - c, y, from_y))

    place = (
        lax.broadcasted_iota(jnp.int32, (tok, 128), 1)
        == lax.broadcasted_iota(jnp.int32, (tok, 128), 0) + tok * c
    ).astype(F32).astype(BF16)
    for copy in small:
        copy.wait()
    meta_own[0:top, :] = jnp.dot(
        ids_ref[...].astype(F32).astype(BF16), place, preferred_element_type=F32
    )
    meta_own[4:4 + top, :] = jnp.dot(probs_ref[...], place, preferred_element_type=F32)

    for i in range(2):
        for copy in loads[i]:
            copy.wait()

        @pl.loop(0, half // 32)
        def _(j):
            part = pl.ds(pl.multiple_of(i * half + j * 32, 32), 32)
            for at in range(0, width, 128):
                lanes = slice(at, at + 128)
                hidden, gate_factor, up_factor = silu_factors(
                    gate_v[part, lanes].astype(F32), up_v[part, lanes].astype(F32)
                )
                hid[x, part, lanes] = hidden.astype(BF16)
                a_gate[part, lanes] = gate_factor
                a_up[part, lanes] = up_factor

    peers = experts - 1 + RING * RING - 1
    pl.semaphore_wait(barrier, peers + jnp.where(gives_home, 0, 1) + jnp.where(takes_home, 0, 1))

    def swap(core):
        device = (2 * z + core, share(core), x)
        return (
            pltpu.make_async_remote_copy(
                src_ref=meta_own, dst_ref=meta_in.at[c], send_sem=ms.at[core],
                recv_sem=mr.at[c], device_id=device, device_id_type=MESH,
            ),
            pltpu.make_async_remote_copy(
                src_ref=og_v.at[core], dst_ref=x2.at[c], send_sem=xs.at[core],
                recv_sem=xr.at[c], device_id=device, device_id_type=MESH,
            ),
        )

    for core in range(2):
        at_home = jnp.logical_and(stays, c == core)

        @pl.when(at_home)
        def _():
            local(meta_own, meta_in.at[c], mr.at[c]).start()
            local(og_v.at[core], x2.at[c], xr.at[c]).start()

        @pl.when(jnp.logical_not(at_home))
        def _():
            for copy in swap(core):
                copy.start()

    part_a, part_e = pl.ds(0, quarter), pl.ds(quarter, quarter)
    eighth = quarter // 2
    part_c, part_d = pl.ds(quarter, eighth), pl.ds(quarter + eighth, eighth)
    far_a = pl.ds(half, quarter)
    far_c, far_d = (pl.ds(half + quarter + i * eighth, eighth) for i in range(2))

    def pass_hidden(index, block, part, to_right):
        at = hid.at[block, part]
        return pltpu.make_async_remote_copy(
            src_ref=at, dst_ref=at, send_sem=hs.at[index], recv_sem=hr.at[index],
            device_id=(e, x_right if to_right else x_left, y), device_id_type=MESH,
        )

    h_r0 = pass_hidden(0, x, first, True)
    h_r1 = pass_hidden(1, x, second, True)
    h_l0 = pass_hidden(2, x, first, False)
    h_l1 = pass_hidden(3, x, second, False)
    h_ra = pass_hidden(4, x_left, part_a, True)
    h_la = pass_hidden(5, x_right, far_a, False)
    h_rc = pass_hidden(6, x_left, part_c, True)
    h_lc = pass_hidden(7, x_right, far_c, False)
    h_rd = pass_hidden(8, x_left, part_d, True)
    h_ld = pass_hidden(9, x_right, far_d, False)
    for copy in (h_r0, h_l1, h_r1, h_l0):
        copy.start()
    for core in range(2):
        local(meta_own, meta_in.at[core], mr.at[core]).wait()
        local(x2.at[core], x2.at[core], xr.at[core]).wait()
    meta = meta_in[0] + meta_in[1]
    lane = lax.broadcasted_iota(jnp.int32, (experts, 128), 1)
    expert_row = lax.broadcasted_iota(jnp.int32, (experts, 128), 0).astype(F32)
    member = jnp.zeros((experts, 128), F32)
    scale = jnp.zeros((experts, 128), F32)
    for k in range(top):
        named = meta[k:k + 1, :] == expert_row
        member = jnp.where(named, 1.0, member)
        scale = jnp.where(named, meta[4 + k:5 + k, :], scale)
    live = lane < 2 * tok
    member = jnp.where(live, member, 0.0)
    row_i = lax.broadcasted_iota(jnp.int32, (128, 128), 0)
    lane_i = lax.broadcasted_iota(jnp.int32, (128, 128), 1)
    before = jnp.logical_and(row_i < lane_i, jnp.logical_or(row_i >= tok, lane_i < tok))
    earlier = jnp.dot(
        member.astype(BF16), before.astype(F32).astype(BF16), preferred_element_type=F32
    )
    target = jnp.where(
        member > 0.0, earlier + jnp.where(lane >= tok, float(cap), 0.0), -1.0
    )
    slot_row = lax.broadcasted_iota(jnp.int32, (experts, pair, 128), 1).astype(F32)
    pick = jnp.where(slot_row == target[:, None, :], scale[:, None, :], 0.0).astype(BF16)
    sb[...] = jnp.dot(
        pick.reshape(experts * pair, 128)[:, :2 * tok], x2[...].reshape(2 * tok, lanes_half),
        preferred_element_type=F32,
    ).astype(BF16)
    my_rows = pl.ds(pl.multiple_of(pair * z, 16), pair)
    my_lanes = pl.ds(pl.multiple_of(lanes_half * c, 128), lanes_half)

    def dispatch(to):
        return pltpu.make_async_remote_copy(
            src_ref=sb.at[pl.ds(pl.multiple_of(pair * to, 16), pair)],
            dst_ref=rows.at[y, my_rows, my_lanes],
            send_sem=zs.at[to], recv_sem=zr.at[e],
            device_id=(to, x, y), device_id_type=MESH,
        )

    chips = experts // 2

    def chip(j):
        away = lax.div(j + 1, 2)
        return lax.rem(jnp.where(lax.rem(j, 2) == 1, z + away, z - away + chips), chips)

    local(
        sb.at[pl.ds(pl.multiple_of(pair * e, 16), pair)], rows.at[y, my_rows, my_lanes], zr.at[e]
    ).start()
    dispatch(2 * z + 1 - c).start()

    def dispatch_both(j):
        for core in range(2):
            dispatch(2 * chip(j) + core).start()

    @pl.loop(1, chips)
    def _(j):
        dispatch_both(j)

    def pass_rows(j, block, to_right, index):
        at = rows.at[block, pl.ds(pl.multiple_of(pair * chip(j), 16), pair)]
        return pltpu.make_async_remote_copy(
            src_ref=at, dst_ref=at, send_sem=ys.at[index], recv_sem=yr.at[index],
            device_id=(e, x, y_right if to_right else y_left), device_id_type=MESH,
        )

    def go_right(j):
        return pass_rows(j, y, True, j)

    def go_left(j):
        return pass_rows(j, y, False, chips + j)

    def on_right(j):
        return pass_rows(j, y_left, True, 2 * chips + j)

    def on_left(j):
        return pass_rows(j, y_right, False, 2 * chips + j)

    def start_own(j):
        for core in range(2):
            at = rows.at[
                y, pl.ds(pl.multiple_of(pair * chip(j), 16), pair),
                pl.ds(lanes_half * core, lanes_half),
            ]
            local(at, at, zr.at[2 * chip(j) + core]).wait()
        go_right(j).start()
        go_left(j).start()

    def start_on(j):
        go_right(j).wait_recv()
        go_left(j).wait_recv()

        (on_right, on_left)[j % 2](j).start()

    tiles = [(at, min(256, width - at)) for at in range(0, width, 256)]

    def send(index, src, dst, to_right):
        return pltpu.make_async_remote_copy(
            src_ref=src, dst_ref=dst, send_sem=bs.at[index], recv_sem=br.at[index],
            device_id=(e, x_right if to_right else x_left, y), device_id_type=MESH,
        )

    far0 = send(0, part_b.at[2, 0], rb_o.at[0], True)
    far1 = send(1, part_b.at[2, 1], rb_o.at[1], False)
    near0, near1 = (
        [
            send(8 + 2 * i + k, part_b.at[role, 1 - k, part], rb_d.at[k, part], k == 0)
            for i, part in enumerate((part_a, part_e))
        ]
        for k, role in enumerate((1, 3))
    )
    both = [
        (send(4 + 2 * i, sb_c.at[0, part], rb_c.at[0, part], True),
         send(5 + 2 * i, sb_c.at[1, part], rb_c.at[1, part], False))
        for i, part in enumerate((part_a, part_e))
    ]

    def partial(replica):
        role = lax.rem(replica - x + RING, RING)
        block = rows[replica]
        for at, size in tiles:
            product = jnp.dot(block, w_v[:, at:at + size], preferred_element_type=F32)
            for i in range(2):
                value = product[i * half:(i + 1) * half]
                part_f[role, i, :, at:at + size] = value
                part_b[role, i, :, at:at + size] = value.astype(BF16)

        @pl.when(role == 2)
        def _():
            far0.start()
            far1.start()

        @pl.when(role == 1)
        def _():
            near0[0].start()

        @pl.when(role == 3)
        def _():
            near1[0].start()

    for j in range(chips):
        start_own(j)

    @pl.when(x == y)
    def _():
        h_r0.wait_recv()
        h_rc.start()
        h_l1.wait_recv()
        h_lc.start()

    load_w.wait()
    partial(y)

    for k in range(chips):
        start_on(k)

    partial(jnp.where(x == y_right, y_left, y_right))
    partial(jnp.where(x == y_right, y_right, y_left))

    @pl.loop(0, chips)
    def _(j):
        @pl.when(lax.rem(j, 2) == 0)
        def _():
            on_right(j).wait_recv()

        @pl.when(lax.rem(j, 2) == 1)
        def _():
            on_left(j).wait_recv()

    partial(y_far)
    near0[1].start()
    near1[1].start()

    @pl.when(x != y)
    def _():
        h_r0.wait_recv()
        h_l1.wait_recv()

    for copy in (h_r1, h_l0):
        copy.wait_recv()
    step = 256 if features % 256 == 0 else 128

    def outer(block, slot_parts, at):
        left = jnp.concatenate([rows[block, p, at:at + step] for p in slot_parts], axis=0)
        right = jnp.concatenate([hid[block, p, :] for p in slot_parts], axis=0)
        return lax.dot_general(
            left, right, (((0,), (0,)), ((), ())), preferred_element_type=F32
        )

    everything = (slice(0, slots),)
    for at in range(0, features, step):
        wg_acc[at:at + step, :] = (
            outer(x, everything, at) + outer(x_left, everything, at) + outer(x_right, everything, at)
        )
    early = (slice(0, quarter), slice(half, half + quarter))
    late = [
        tuple(slice(at + i * eighth, at + (i + 1) * eighth) for at in (quarter, half + quarter))
        for i in range(2)
    ]

    for core in range(2):
        @pl.when(jnp.logical_not(jnp.logical_and(stays, c == core)))
        def _():
            for copy in swap(core):
                copy.wait_send()

    @pl.loop(1, experts)
    def _(i):
        dispatch(lax.rem(e + i, experts)).wait_send()

    @pl.loop(0, chips)
    def _(j):
        go_right(j).wait_send()
        go_left(j).wait_send()

        @pl.when(lax.rem(j, 2) == 0)
        def _():
            on_right(j).wait_send()

        @pl.when(lax.rem(j, 2) == 1)
        def _():
            on_left(j).wait_send()

    def pass_on(side):
        @pl.when(side == 0)
        def _():
            far0.wait_recv()

        @pl.when(side == 1)
        def _():
            far1.wait_recv()

        for i in range(2):
            @pl.loop(0, quarter // 16)
            def _(j):
                part = pl.ds(pl.multiple_of(i * quarter + j * 16, 16), 16)
                sb_c[side, part, :] = (
                    part_f[1 + 2 * side, side, part, :] + rb_o[side, part, :].astype(F32)
                ).astype(BF16)

            for k in range(2):
                @pl.when(side == k)
                def _():
                    both[i][k].start()

        @pl.when(side == 0)
        def _():
            h_ra.start()

        @pl.when(side == 1)
        def _():
            h_la.start()

        @pl.when(jnp.logical_and(side == 0, x != y))
        def _():
            h_rc.start()

        @pl.when(jnp.logical_and(side == 1, x != y))
        def _():
            h_lc.start()

    early_side = jnp.where(x_left == y, 1, 0)
    pass_on(early_side)
    pass_on(1 - early_side)
    for copy in near0 + near1:
        copy.wait_recv()

    zero = jnp.zeros((16, 128), F32)
    peaks = (zero, zero)
    for i, pair_of in enumerate(both):
        for copy in pair_of:
            copy.wait_recv()
        for side in range(2):
            def body(j, carry):
                gate_peak, up_peak = carry
                part = pl.ds(pl.multiple_of(i * quarter + j * 16, 16), 16)
                at = pl.ds(pl.multiple_of(side * half + i * quarter + j * 16, 16), 16)
                sent = rb_d[1 - side, part, :].astype(F32) + rb_c[side, part, :].astype(F32)
                d_hidden = part_f[0, side, part, :] + sent
                gate_delta = d_hidden * a_gate[at, :]
                up_delta = d_hidden * a_up[at, :]
                a_gate[at, :] = gate_delta
                a_up[at, :] = up_delta
                weighted = up_delta * up_v[at, :].astype(F32)
                total = zero
                for lane0 in range(0, width, 128):
                    sl = slice(lane0, lane0 + 128)
                    gate_peak = jnp.maximum(gate_peak, jnp.abs(gate_delta[:, sl]))
                    up_peak = jnp.maximum(up_peak, jnp.abs(up_delta[:, sl]))
                    total = total + weighted[:, sl]
                rl[at, :] = total
                return gate_peak, up_peak

            peaks = lax.fori_loop(0, quarter // 16, body, peaks)
    peak_row = lax.broadcasted_iota(jnp.int32, (8, 128), 0)
    pk_own[...] = jnp.where(
        peak_row < 4,
        jnp.max(peaks[0], axis=0, keepdims=True), jnp.max(peaks[1], axis=0, keepdims=True),
    )

    def tell_row(p):
        return pltpu.make_async_remote_copy(
            src_ref=pk_own, dst_ref=pk_in.at[y], send_sem=ps.at[p], recv_sem=pr.at[y],
            device_id=(e, x, p), device_id_type=MESH,
        )

    def tell_column(p):
        return pltpu.make_async_remote_copy(
            src_ref=pk_row, dst_ref=pk_rows.at[x], send_sem=qs.at[p], recv_sem=qr.at[x],
            device_id=(e, p, y), device_id_type=MESH,
        )

    y_others, x_others = (y_right, y_left, y_far), (x_right, x_left, x_far)
    for p in y_others:
        tell_row(p).start()

    rl[slots:, :] = jnp.zeros((rl.shape[0] - slots, 128), F32)
    ones = jnp.ones((8, 128), BF16)
    across = (((1,), (1,)), ((), ()))

    def split(value):
        high = value.astype(BF16)
        return high, (value - high.astype(F32)).astype(BF16)

    sums = sum(
        lax.dot_general(ones, part, across, preferred_element_type=F32) for part in split(rl[...])
    )
    rz_out[...] = sums[0:1, :]

    def give_back(to):
        return pltpu.make_async_remote_copy(
            src_ref=rz_out, dst_ref=rz_in.at[e], send_sem=ws.at[to], recv_sem=wr.at[e],
            device_id=(to, x, y), device_id_type=MESH,
        )

    @pl.loop(1, experts)
    def _(i):
        give_back(lax.rem(e + i, experts)).start()

    rz_in[e] = rz_out[...]
    row_peak = pk_own[...]
    for p in y_others:
        local(pk_in.at[p], pk_in.at[p], pr.at[p]).wait()
        row_peak = jnp.maximum(row_peak, pk_in[p])
    pk_row[...] = row_peak
    for p in x_others:
        tell_column(p).start()
    h_rd.start()
    h_ld.start()
    @pl.loop(1, experts)
    def _(i):
        s = lax.rem(e + i, experts)
        local(rz_in.at[s], rz_in.at[s], wr.at[s]).wait()

    from_experts = rz_in[:, 0, :]
    mine = (
        lax.broadcasted_iota(jnp.int32, (128, from_experts.shape[1]), 1)
        == lax.broadcasted_iota(jnp.int32, (128, from_experts.shape[1]), 0) + cap * e
    ).astype(F32).astype(BF16)
    ry_own[...] = sum(
        lax.dot_general(part, mine, across, preferred_element_type=F32)
        for part in split(from_experts)
    )

    def tell_sum(p):
        return pltpu.make_async_remote_copy(
            src_ref=ry_own, dst_ref=ry_in.at[y], send_sem=vs.at[p], recv_sem=vr.at[y],
            device_id=(e, x, p), device_id_type=MESH,
        )

    for p in y_others:
        tell_sum(p).start()

    for copy in (h_ra, h_la):
        copy.wait_recv()
    for at in range(0, features, step):
        wg_acc[at:at + step, :] += outer(x_far, early, at)

    all_peaks = row_peak
    for p in x_others:
        local(pk_rows.at[p], pk_rows.at[p], qr.at[p]).wait()
        all_peaks = jnp.maximum(all_peaks, pk_rows[p])
    gate_scale = 1.0 / (jnp.max(all_peaks[:4], axis=(0, 1), keepdims=True) + 1e-6)
    up_scale = 1.0 / (jnp.max(all_peaks[4:], axis=(0, 1), keepdims=True) + 1e-6)

    @pl.loop(0, slots // 16)
    def _(j):
        part = pl.ds(pl.multiple_of(j * 16, 16), 16)
        gate_out[part, :] = (a_gate[part, :] * gate_scale).astype(BF16)
        up_out[part, :] = (a_up[part, :] * up_scale).astype(BF16)

    for copy in (h_rc, h_lc):
        copy.wait_recv()
    for at in range(0, features, step):
        wg_acc[at:at + step, :] += outer(x_far, late[0], at)


    ids_f = ids_ref[...].astype(F32)
    expert_col = lax.broadcasted_iota(jnp.int32, (experts, tok), 0).astype(F32)
    named = [(ids_f[k:k + 1, :] == expert_col).astype(F32) for k in range(top)]
    tri = (
        lax.broadcasted_iota(jnp.int32, (tok, tok), 0)
        < lax.broadcasted_iota(jnp.int32, (tok, tok), 1)
    ).astype(F32).astype(BF16)
    earlier = jnp.dot(sum(named).astype(BF16), tri, preferred_element_type=F32)
    slot_col = lax.broadcasted_iota(jnp.int32, (128, tok), 0).astype(F32)
    at_slot = [
        slot_col == jnp.sum(earlier * named[k], axis=0, keepdims=True) for k in range(top)
    ]
    for p in y_others:
        local(ry_in.at[p], ry_in.at[p], vr.at[p]).wait()
    sums = ry_own[...]
    for p in y_others:
        sums = sums + ry_in[p]
    high, low = split(sums)
    down = (((0,), (0,)), ((), ()))
    for k in range(top):
        pick = named[k].astype(BF16)
        found = lax.dot_general(
            high, pick, down, preferred_element_type=F32
        ) + lax.dot_general(low, pick, down, preferred_element_type=F32)
        value = jnp.sum(jnp.where(at_slot[k], found, 0.0), axis=0, keepdims=True)
        router_out[k:k + 1, :] = value / probs_ref[k:k + 1, :].astype(F32)

    for copy in (h_rd, h_ld):
        copy.wait_recv()
    for at in range(0, features, step):
        wg_out[at:at + step, :] = (wg_acc[at:at + step, :] + outer(x_far, late[1], at)).astype(BF16)

    @pl.loop(1, experts)
    def _(i):
        to = lax.rem(e + i, experts)
        give_back(to).wait_send()

    for p in y_others:
        tell_sum(p).wait_send()
        tell_row(p).wait_send()
    for p in x_others:
        tell_column(p).wait_send()
    for copy in (h_r0, h_r1, h_l0, h_l1, h_ra, h_la, h_rc, h_lc, h_rd, h_ld):
        copy.wait_send()

    for copy in [far0, far1] + near0 + near1 + list(both[0] + both[1]):
        copy.wait_send()


def write_out(*refs):
    count = len(refs) // 2
    copies = [local(refs[i], refs[count + i], refs[-1].at[i]) for i in range(count)]
    for copy in copies:
        copy.start()
    for copy in copies:
        copy.wait()


def shards(out_grad, router_probs, expert_ids, saved_gate, saved_up, down_weight):
    tok, top = expert_ids.shape
    experts = lax.axis_size("expert")
    cap = saved_gate.shape[3]
    width = saved_gate.shape[4]
    slots = saved_gate.shape[2] * cap
    features = down_weight.shape[1]
    half = slots // 2
    chips = experts // 2
    any_space = pl.BlockSpec(memory_space=pl.ANY)
    hbm = pl.BlockSpec(memory_space=pltpu.HBM)
    vmem = pl.BlockSpec(memory_space=pltpu.VMEM)
    dma = pltpu.SemaphoreType.DMA
    stay = functools.partial(pltpu.with_memory_space_constraint, memory_space=pltpu.HBM)
    shapes = (
        ((slots, width), BF16), ((slots, width), BF16), ((features, width), BF16),
        ((top, tok), F32),
    )
    results = pl.pallas_call(
        functools.partial(kernel, experts, cap, tok, top),
        out_shape=tuple(pltpu.VMEM(*shape) for shape in shapes),
        in_specs=[hbm] * 6,
        out_specs=(vmem,) * 4,
        scratch_shapes=[
            pltpu.VMEM((top, tok), jnp.int32),
            pltpu.VMEM((top, tok), BF16),
            pltpu.VMEM((2, tok, features // 2), BF16),
            pltpu.VMEM((slots, width), BF16),
            pltpu.VMEM((slots, width), BF16),
            pltpu.VMEM((features, width), BF16),
            pltpu.VMEM((slots, width), F32),
            pltpu.VMEM((slots, width), F32),
            pltpu.VMEM((RING, slots, width), BF16),
            pltpu.VMEM((RING, slots, features), BF16),
            pltpu.VMEM((2, tok, features // 2), BF16),
            pltpu.VMEM((8, 128), F32),
            pltpu.VMEM((2, 8, 128), F32),
            pltpu.VMEM((2 * cap * experts, features // 2), BF16),
            pltpu.VMEM((RING, 2, half, width), F32),
            pltpu.VMEM((RING, 2, half, width), BF16),
            pltpu.VMEM((2, half, width), BF16),
            pltpu.VMEM((2, half, width), BF16),
            pltpu.VMEM((2, half, width), BF16),
            pltpu.VMEM((2, half, width), BF16),
            pltpu.VMEM((features, width), F32),
            pltpu.VMEM((8, 128), F32),
            pltpu.VMEM((RING, 8, 128), F32),
            pltpu.VMEM((8, 128), F32),
            pltpu.VMEM((RING, 8, 128), F32),
            pltpu.VMEM((slots + 128, 128), F32),
            pltpu.VMEM((1, slots + 128), F32),
            pltpu.VMEM((experts, 1, slots + 128), F32),
            pltpu.VMEM((experts, 128), F32),
            pltpu.VMEM((RING, experts, 128), F32),
            dma((9,)),
            dma((2,)), dma((2,)), dma((2,)), dma((2,)),
            dma((experts,)), dma((experts,)),
            dma((3 * chips,)), dma((3 * chips,)),
            dma((10,)), dma((10,)),
            dma((12,)), dma((12,)),
            dma((RING,)), dma((RING,)), dma((RING,)), dma((RING,)),
            dma((experts,)), dma((experts,)),
            dma((RING,)), dma((RING,)),
        ],
        compiler_params=pltpu.CompilerParams(
            collective_id=0, has_side_effects=True, vmem_limit_bytes=48 * 1024 * 1024
        ),
        cost_estimate=pl.CostEstimate(
            flops=4 * RING * slots * features * width,
            bytes_accessed=4 * slots * width + 2 * features * width,
            transcendentals=slots * width,
        ),
    )(
        stay(out_grad), stay(expert_ids.T), stay(router_probs.T), stay(saved_gate.reshape(slots, width)),
        stay(saved_up.reshape(slots, width)), stay(down_weight.reshape(features, width)),
    )
    gate_grad, up_grad, weight_grad, router_grad = pl.pallas_call(
        write_out,
        out_shape=tuple(jax.ShapeDtypeStruct(*shape) for shape in shapes),
        in_specs=[vmem] * 4,
        out_specs=(any_space,) * 4,
        scratch_shapes=[dma((4,))],
        compiler_params=pltpu.CompilerParams(vmem_limit_bytes=1024 * 1024),
    )(*(pltpu.with_memory_space_constraint(r, memory_space=pltpu.VMEM) for r in results))
    return (
        gate_grad.reshape(saved_gate.shape), up_grad.reshape(saved_up.shape),
        weight_grad.reshape(down_weight.shape), router_grad.T,
    )


def solution(mesh):
    in_specs = (
        P(("expert", "edata"), None),
        P(("expert", "edata"), None),
        P(("expert", "edata"), None),
        P("expert", "edata", None, None, "tensor"),
        P("expert", "edata", None, None, "tensor"),
        P("expert", "edata", "tensor"),
    )
    out_specs = (
        P("expert", "edata", None, None, "tensor"),
        P("expert", "edata", None, None, "tensor"),
        P("expert", "edata", "tensor"),
        P(("expert", "edata"), None),
    )
    return jax.shard_map(shards, mesh=mesh, in_specs=in_specs, out_specs=out_specs, check_vma=False)
```

```python
import functools

import jax
import jax.numpy as jnp
from jax import lax
from jax.experimental import pallas as pl
from jax.experimental.pallas import tpu as pltpu
from jax.sharding import PartitionSpec as P

MESH = pl.DeviceIdType.MESH
RING = 4
F32 = jnp.float32
BF16 = jnp.bfloat16


def local(src, dst, sem):
    return pltpu.make_async_copy(src, dst, sem)


def landed(ref, sem):
    pltpu.make_async_copy(ref, ref, sem).wait()


def silu_factors(gate_value, up_value):
    sigmoid_gate = jax.nn.sigmoid(gate_value)
    activated = gate_value * sigmoid_gate
    gate_factor = up_value * sigmoid_gate * (1.0 + gate_value * (1.0 - sigmoid_gate))
    return activated * up_value, gate_factor, activated


def kernel(
    experts, cap, tok, top,
    og, ids, probs, gate, up, w,
    a_gate, a_up, wg_acc, late_rows, late_hid, scales, router_out,
    ids_ref, probs_ref, og_v, gate_v, up_v, w_v, hid, rows, x2, meta_own, meta_in, sb,
    part_f, part_b, sb_c, rb_o, rb_d, rb_c,
    pk_own, pk_in, pk_row, pk_rows, rl, rz_out, rz_in, ry_own, ry_in,
    load_sem, xs, xr, ms, mr, zs, zr, ys, yr, hs, hr, bs, br, ps, pr, qs, qr, ws, wr, vs, vr,
):
    e, x, y = lax.axis_index("expert"), lax.axis_index("edata"), lax.axis_index("tensor")
    z, c = lax.div(e, 2), lax.rem(e, 2)
    slots, width = gate.shape
    half = slots // 2
    quarter = half // 2
    features = w.shape[0]
    lanes_half = features // 2
    pair = 2 * cap
    x_right, x_left, x_far = lax.rem(x + 1, RING), lax.rem(x + 3, RING), lax.rem(x + 2, RING)
    y_right, y_left, y_far = lax.rem(y + 1, RING), lax.rem(y + 3, RING), lax.rem(y + 2, RING)
    first, second = pl.ds(0, half), pl.ds(half, half)
    fill_right = jnp.logical_or(x == y, x_left == y)
    fill_left = jnp.logical_or(x == y, x_right == y)

    def share(core):
        return lax.rem(y - x + 2 * core + RING, RING)

    from_y = lax.rem(x + y + 2 * c, RING)
    gives_home = jnp.logical_and(share(1 - c) == x, x == y)
    takes_home = jnp.logical_and(from_y == y, x == y)
    stays = jnp.logical_and(share(c) == x, x == y)

    loads = [
        tuple(
            local(ref.at[part], held.at[part], load_sem.at[6 + 2 * i + k])
            for k, (ref, held) in enumerate(((gate, gate_v), (up, up_v)))
        )
        for i, part in enumerate((first, second))
    ]
    load_w = local(w, w_v, load_sem.at[2])
    small = (
        local(ids, ids_ref, load_sem.at[3]),
        local(probs, probs_ref, load_sem.at[4]),
    )
    tokens = tuple(
        local(
            og.at[:, pl.ds(
                pl.multiple_of(features * share(core) + lanes_half * core, 128), lanes_half
            )],
            og_v.at[core], load_sem.at[5],
        )
        for core in range(2)
    )
    for copy in small + tokens:
        copy.start()
    for copy in loads[0] + loads[1]:
        copy.start()
    load_w.start()

    barrier = pltpu.get_barrier_semaphore()

    def greet(device):
        pl.semaphore_signal(barrier, inc=1, device_id=device, device_id_type=MESH)

    @pl.loop(1, experts)
    def _(i):
        greet((lax.rem(e + i, experts), x, y))

    @pl.loop(1, RING * RING)
    def _(i):
        p = lax.rem(x * RING + y + i, RING * RING)
        greet((e, lax.div(p, RING), lax.rem(p, RING)))

    @pl.when(jnp.logical_not(gives_home))
    def _():
        greet((2 * z + 1 - c, share(1 - c), x))

    @pl.when(jnp.logical_not(takes_home))
    def _():
        greet((2 * z + 1 - c, y, from_y))

    place = (
        lax.broadcasted_iota(jnp.int32, (tok, 128), 1)
        == lax.broadcasted_iota(jnp.int32, (tok, 128), 0) + tok * c
    ).astype(F32).astype(BF16)
    for copy in small:
        copy.wait()
    meta_own[0:top, :] = jnp.dot(
        ids_ref[...].astype(F32).astype(BF16), place, preferred_element_type=F32
    )
    meta_own[4:4 + top, :] = jnp.dot(probs_ref[...], place, preferred_element_type=F32)

    def hidden_of(i):
        for copy in loads[i]:
            copy.wait()

        @pl.loop(0, half // 32)
        def _(j):
            part = pl.ds(pl.multiple_of(i * half + j * 32, 32), 32)
            for at in range(0, width, 128):
                lanes = slice(at, at + 128)
                hidden, gate_factor, up_factor = silu_factors(
                    gate_v[part, lanes].astype(F32), up_v[part, lanes].astype(F32)
                )
                hid[x, part, lanes] = hidden.astype(BF16)
                a_gate[part, lanes] = gate_factor
                a_up[part, lanes] = up_factor

    landed(og_v, load_sem.at[5])
    hidden_of(0)
    peers = experts - 1 + RING * RING - 1
    pl.semaphore_wait(barrier, peers + jnp.where(gives_home, 0, 1) + jnp.where(takes_home, 0, 1))

    def swap(core):
        device = (2 * z + core, share(core), x)
        return (
            pltpu.make_async_remote_copy(
                src_ref=meta_own, dst_ref=meta_in.at[c], send_sem=ms.at[core],
                recv_sem=mr.at[c], device_id=device, device_id_type=MESH,
            ),
            pltpu.make_async_remote_copy(
                src_ref=og_v.at[core], dst_ref=x2.at[c], send_sem=xs.at[core],
                recv_sem=xr.at[c], device_id=device, device_id_type=MESH,
            ),
        )

    for core in range(2):
        at_home = jnp.logical_and(stays, c == core)

        @pl.when(at_home)
        def _():
            local(meta_own, meta_in.at[c], mr.at[c]).start()
            local(og_v.at[core], x2.at[c], xr.at[c]).start()

        @pl.when(jnp.logical_not(at_home))
        def _():
            for copy in swap(core):
                copy.start()

    part_a, part_e = pl.ds(0, quarter), pl.ds(quarter, quarter)
    last = quarter // 3
    more = quarter - last
    part_c, part_d = pl.ds(quarter, more), pl.ds(quarter + more, last)
    far_a = pl.ds(half, quarter)
    far_c, far_d = pl.ds(half + quarter, more), pl.ds(half + quarter + more, last)

    def pass_hidden(index, block, part, to_right):
        at = hid.at[block, part]
        return pltpu.make_async_remote_copy(
            src_ref=at, dst_ref=at, send_sem=hs.at[0], recv_sem=hr.at[index],
            device_id=(e, x_right if to_right else x_left, y), device_id_type=MESH,
        )

    h_r0 = pass_hidden(0, x, first, True)
    h_r1 = pass_hidden(2, x, second, True)
    h_l0 = pass_hidden(2, x, first, False)
    h_l1 = pass_hidden(1, x, second, False)
    h_ra = pass_hidden(3, x_left, part_a, True)
    h_la = pass_hidden(3, x_right, far_a, False)
    h_rc = pass_hidden(4, x_left, part_c, True)
    h_lc = pass_hidden(4, x_right, far_c, False)
    h_rd = pass_hidden(5, x_left, part_d, True)
    h_ld = pass_hidden(5, x_right, far_d, False)
    h_r0.start()
    hidden_of(1)
    for copy in (h_l1, h_r1, h_l0):
        copy.start()
    for core in range(2):
        local(meta_own, meta_in.at[core], mr.at[core]).wait()
        local(x2.at[core], x2.at[core], xr.at[core]).wait()
    meta = meta_in[0] + meta_in[1]
    lane = lax.broadcasted_iota(jnp.int32, (experts, 128), 1)
    expert_row = lax.broadcasted_iota(jnp.int32, (experts, 128), 0).astype(F32)
    member = jnp.zeros((experts, 128), F32)
    scale = jnp.zeros((experts, 128), F32)
    for k in range(top):
        named = meta[k:k + 1, :] == expert_row
        member = jnp.where(named, 1.0, member)
        scale = jnp.where(named, meta[4 + k:5 + k, :], scale)
    live = lane < 2 * tok
    member = jnp.where(live, member, 0.0)
    row_i = lax.broadcasted_iota(jnp.int32, (128, 128), 0)
    lane_i = lax.broadcasted_iota(jnp.int32, (128, 128), 1)
    before = jnp.logical_and(row_i < lane_i, jnp.logical_or(row_i >= tok, lane_i < tok))
    earlier = jnp.dot(
        member.astype(BF16), before.astype(F32).astype(BF16), preferred_element_type=F32
    )
    target = jnp.where(
        member > 0.0, earlier + jnp.where(lane >= tok, float(cap), 0.0), -1.0
    )
    slot_row = lax.broadcasted_iota(jnp.int32, (experts, pair, 128), 1).astype(F32)
    pick = jnp.where(slot_row == target[:, None, :], scale[:, None, :], 0.0).astype(BF16)
    sb[...] = jnp.dot(
        pick.reshape(experts * pair, 128)[:, :2 * tok], x2[...].reshape(2 * tok, lanes_half),
        preferred_element_type=F32,
    ).astype(BF16)
    my_rows = pl.ds(pl.multiple_of(pair * z, 16), pair)
    my_lanes = pl.ds(pl.multiple_of(lanes_half * c, 128), lanes_half)

    def dispatch(to):
        return pltpu.make_async_remote_copy(
            src_ref=sb.at[pl.ds(pl.multiple_of(pair * to, 16), pair)],
            dst_ref=rows.at[y, my_rows, my_lanes],
            send_sem=zs.at[0], recv_sem=zr.at[z],
            device_id=(to, x, y), device_id_type=MESH,
        )

    chips = experts // 2

    def chip(j):
        away = lax.div(j + 1, 2)
        return lax.rem(jnp.where(lax.rem(j, 2) == 1, z + away, z - away + chips), chips)

    local(
        sb.at[pl.ds(pl.multiple_of(pair * e, 16), pair)], rows.at[y, my_rows, my_lanes], zr.at[z]
    ).start()
    dispatch(2 * z + 1 - c).start()

    def dispatch_both(j):
        for core in range(2):
            dispatch(2 * chip(j) + core).start()

    @pl.loop(1, chips)
    def _(j):
        dispatch_both(j)

    def pass_rows(j, block, to_right, sem):
        at = rows.at[block, pl.ds(pl.multiple_of(pair * chip(j), 16), pair)]
        return pltpu.make_async_remote_copy(
            src_ref=at, dst_ref=at, send_sem=ys.at[0], recv_sem=yr.at[sem],
            device_id=(e, x, y_right if to_right else y_left), device_id_type=MESH,
        )

    def go_right(j):
        return pass_rows(j, y, True, j)

    def go_left(j):
        return pass_rows(j, y, False, j)

    def on_right(j):
        return pass_rows(j, y_left, True, chips)

    def on_left(j):
        return pass_rows(j, y_right, False, chips)

    def start_own(j):
        landed(
            rows.at[y, pl.ds(pl.multiple_of(pair * chip(j), 16), pair)], zr.at[chip(j)]
        )
        go_right(j).start()
        go_left(j).start()

    def start_on(j):
        landed(rows.at[pl.ds(0, 2), pl.ds(0, pair)], yr.at[j])

        (on_right, on_left)[j % 2](j).start()

    tiles = [(at, min(256, width - at)) for at in range(0, width, 256)]

    def send(index, src, dst, to_right):
        return pltpu.make_async_remote_copy(
            src_ref=src, dst_ref=dst, send_sem=bs.at[0], recv_sem=br.at[index],
            device_id=(e, x_right if to_right else x_left, y), device_id_type=MESH,
        )

    far0 = send(0, part_b.at[2, 0], rb_o.at[0], True)
    far1 = send(1, part_b.at[2, 1], rb_o.at[1], False)
    near0, near1 = (
        [
            send(2, part_b.at[role, 1 - k, part], rb_d.at[k, part], k == 0)
            for part in (part_a, part_e)
        ]
        for k, role in enumerate((1, 3))
    )
    both = [
        (send(3 + i, sb_c.at[0, part], rb_c.at[0, part], True),
         send(3 + i, sb_c.at[1, part], rb_c.at[1, part], False))
        for i, part in enumerate((part_a, part_e))
    ]

    def partial(replica):
        role = lax.rem(replica - x + RING, RING)
        block = rows[replica]
        for at, size in tiles:
            product = jnp.dot(block, w_v[:, at:at + size], preferred_element_type=F32)
            for i in range(2):
                value = product[i * half:(i + 1) * half]
                part_f[role, i, :, at:at + size] = value
                part_b[role, i, :, at:at + size] = value.astype(BF16)

        @pl.when(role == 2)
        def _():
            far0.start()
            far1.start()

        @pl.when(role == 1)
        def _():
            near0[0].start()

        @pl.when(role == 3)
        def _():
            near1[0].start()

    for j in range(chips):
        start_own(j)

    @pl.when(fill_right)
    def _():
        h_r0.wait_recv()
        h_rc.start()

    @pl.when(fill_left)
    def _():
        h_l1.wait_recv()
        h_lc.start()

    load_w.wait()
    partial(y)

    for k in range(chips):
        start_on(k)

    partial(jnp.where(x == y_right, y_left, y_right))
    partial(jnp.where(x == y_right, y_right, y_left))

    landed(rows.at[y_far], yr.at[chips])
    partial(y_far)
    near0[1].start()
    near1[1].start()

    @pl.when(jnp.logical_not(fill_right))
    def _():
        h_r0.wait_recv()

    @pl.when(jnp.logical_not(fill_left))
    def _():
        h_l1.wait_recv()

    landed(hid.at[x], hr.at[2])
    step = 256 if features % 256 == 0 else 128

    def outer(block, slot_parts, at):
        left = jnp.concatenate([rows[block, p, at:at + step] for p in slot_parts], axis=0)
        right = jnp.concatenate([hid[block, p, :] for p in slot_parts], axis=0)
        return lax.dot_general(
            left, right, (((0,), (0,)), ((), ())), preferred_element_type=F32
        )

    everything = (slice(0, slots),)
    for at in range(0, features, step):
        wg_acc[at:at + step, :] = (
            outer(x, everything, at) + outer(x_left, everything, at) + outer(x_right, everything, at)
        )
    early = (slice(0, quarter), slice(half, half + quarter))
    late = tuple(slice(at, at + more) for at in (quarter, half + quarter))
    latest = tuple(slice(at + more, at + quarter) for at in (quarter, half + quarter))

    for core in range(2):
        @pl.when(jnp.logical_not(jnp.logical_and(stays, c == core)))
        def _():
            for copy in swap(core):
                copy.wait_send()

    landed(sb.at[pl.ds(0, pair * (experts - 1))], zs.at[0])
    landed(rows.at[pl.ds(0, 3)], ys.at[0])

    def pass_on(side):
        @pl.when(side == 0)
        def _():
            far0.wait_recv()

        @pl.when(side == 1)
        def _():
            far1.wait_recv()

        for i in range(2):
            @pl.loop(0, quarter // 16)
            def _(j):
                part = pl.ds(pl.multiple_of(i * quarter + j * 16, 16), 16)
                sb_c[side, part, :] = (
                    part_f[1 + 2 * side, side, part, :] + rb_o[side, part, :].astype(F32)
                ).astype(BF16)

            for k in range(2):
                @pl.when(side == k)
                def _():
                    both[i][k].start()

    early_side = jnp.where(x_left == y, 1, 0)
    pass_on(early_side)
    pass_on(1 - early_side)

    h_ra.start()
    h_la.start()

    @pl.when(jnp.logical_not(fill_right))
    def _():
        h_rc.start()

    @pl.when(jnp.logical_not(fill_left))
    def _():
        h_lc.start()

    landed(rb_d, br.at[2])

    zero = jnp.zeros((16, 128), F32)
    peaks = (zero, zero)
    for i in range(2):
        landed(rb_c.at[pl.ds(0, 2), pl.ds(0, quarter)], br.at[3 + i])
        for side in range(2):
            def body(j, carry):
                gate_peak, up_peak = carry
                part = pl.ds(pl.multiple_of(i * quarter + j * 16, 16), 16)
                at = pl.ds(pl.multiple_of(side * half + i * quarter + j * 16, 16), 16)
                sent = rb_d[1 - side, part, :].astype(F32) + rb_c[side, part, :].astype(F32)
                d_hidden = part_f[0, side, part, :] + sent
                gate_delta = d_hidden * a_gate[at, :]
                up_delta = d_hidden * a_up[at, :]
                a_gate[at, :] = gate_delta
                a_up[at, :] = up_delta
                weighted = up_delta * up_v[at, :].astype(F32)
                total = zero
                for lane0 in range(0, width, 128):
                    sl = slice(lane0, lane0 + 128)
                    gate_peak = jnp.maximum(gate_peak, jnp.abs(gate_delta[:, sl]))
                    up_peak = jnp.maximum(up_peak, jnp.abs(up_delta[:, sl]))
                    total = total + weighted[:, sl]
                rl[at, :] = total
                return gate_peak, up_peak

            peaks = lax.fori_loop(0, quarter // 16, body, peaks)
    peak_row = lax.broadcasted_iota(jnp.int32, (8, 128), 0)
    pk_own[...] = jnp.where(
        peak_row < 4,
        jnp.max(peaks[0], axis=0, keepdims=True), jnp.max(peaks[1], axis=0, keepdims=True),
    )

    def tell_row(p):
        return pltpu.make_async_remote_copy(
            src_ref=pk_own, dst_ref=pk_in.at[y], send_sem=ps.at[0], recv_sem=pr.at[0],
            device_id=(e, x, p), device_id_type=MESH,
        )

    def tell_column(p):
        return pltpu.make_async_remote_copy(
            src_ref=pk_row, dst_ref=pk_rows.at[x], send_sem=qs.at[0], recv_sem=qr.at[0],
            device_id=(e, p, y), device_id_type=MESH,
        )

    y_others, x_others = (y_right, y_left, y_far), (x_right, x_left, x_far)
    for p in y_others:
        tell_row(p).start()

    rl[slots:, :] = jnp.zeros((rl.shape[0] - slots, 128), F32)
    ones = jnp.ones((8, 128), BF16)
    across = (((1,), (1,)), ((), ()))

    def split(value):
        high = value.astype(BF16)
        return high, (value - high.astype(F32)).astype(BF16)

    sums = sum(
        lax.dot_general(ones, part, across, preferred_element_type=F32) for part in split(rl[...])
    )
    rz_out[...] = sums[0:1, :]

    def give_back(to):
        return pltpu.make_async_remote_copy(
            src_ref=rz_out, dst_ref=rz_in.at[e], send_sem=ws.at[0], recv_sem=wr.at[0],
            device_id=(to, x, y), device_id_type=MESH,
        )

    @pl.loop(1, experts)
    def _(i):
        give_back(lax.rem(e + i, experts)).start()

    rz_in[e] = rz_out[...]
    row_peak = pk_own[...]
    landed(pk_in.at[pl.ds(0, 3)], pr.at[0])
    for p in y_others:
        row_peak = jnp.maximum(row_peak, pk_in[p])
    pk_row[...] = row_peak
    for p in x_others:
        tell_column(p).start()
    h_rd.start()
    h_ld.start()
    landed(rz_in.at[pl.ds(0, experts - 1)], wr.at[0])
    from_experts = rz_in[:, 0, :]
    mine = (
        lax.broadcasted_iota(jnp.int32, (128, from_experts.shape[1]), 1)
        == lax.broadcasted_iota(jnp.int32, (128, from_experts.shape[1]), 0) + cap * e
    ).astype(F32).astype(BF16)
    ry_own[...] = sum(
        lax.dot_general(part, mine, across, preferred_element_type=F32)
        for part in split(from_experts)
    )

    def tell_sum(p):
        return pltpu.make_async_remote_copy(
            src_ref=ry_own, dst_ref=ry_in.at[y], send_sem=vs.at[0], recv_sem=vr.at[0],
            device_id=(e, x, p), device_id_type=MESH,
        )

    for p in y_others:
        tell_sum(p).start()

    landed(hid.at[x_far, pl.ds(0, 2 * quarter)], hr.at[3])
    for at in range(0, features, step):
        wg_acc[at:at + step, :] += outer(x_far, early, at)

    all_peaks = row_peak
    landed(pk_rows.at[pl.ds(0, 3)], qr.at[0])
    for p in x_others:
        all_peaks = jnp.maximum(all_peaks, pk_rows[p])
    scales[...] = 1.0 / (
        jnp.where(
            peak_row < 4,
            jnp.max(all_peaks[:4], axis=(0, 1), keepdims=True),
            jnp.max(all_peaks[4:], axis=(0, 1), keepdims=True),
        ) + 1e-6
    )
    landed(hid.at[x_far, pl.ds(0, 2 * more)], hr.at[4])
    for at in range(0, features, step):
        wg_acc[at:at + step, :] += outer(x_far, late, at)

    ids_f = ids_ref[...].astype(F32)
    expert_col = lax.broadcasted_iota(jnp.int32, (experts, tok), 0).astype(F32)
    named = [(ids_f[k:k + 1, :] == expert_col).astype(F32) for k in range(top)]
    tri = (
        lax.broadcasted_iota(jnp.int32, (tok, tok), 0)
        < lax.broadcasted_iota(jnp.int32, (tok, tok), 1)
    ).astype(F32).astype(BF16)
    earlier = jnp.dot(sum(named).astype(BF16), tri, preferred_element_type=F32)
    slot_col = lax.broadcasted_iota(jnp.int32, (128, tok), 0).astype(F32)
    at_slot = [
        slot_col == jnp.sum(earlier * named[k], axis=0, keepdims=True) for k in range(top)
    ]
    landed(ry_in.at[pl.ds(0, 3)], vr.at[0])
    sums = ry_own[...]
    for p in y_others:
        sums = sums + ry_in[p]
    high, low = split(sums)
    down = (((0,), (0,)), ((), ()))
    for k in range(top):
        pick = named[k].astype(BF16)
        found = lax.dot_general(
            high, pick, down, preferred_element_type=F32
        ) + lax.dot_general(low, pick, down, preferred_element_type=F32)
        value = jnp.sum(jnp.where(at_slot[k], found, 0.0), axis=0, keepdims=True)
        router_out[k:k + 1, :] = value / probs_ref[k:k + 1, :].astype(F32)

    landed(hid.at[x_far, pl.ds(0, 2 * last)], hr.at[5])
    late_rows[...] = jnp.concatenate([rows[x_far, p, :] for p in latest], axis=0)
    late_hid[...] = jnp.concatenate([hid[x_far, p, :] for p in latest], axis=0)

    landed(rz_in.at[pl.ds(0, experts - 1)], ws.at[0])
    landed(ry_in.at[pl.ds(0, 3)], vs.at[0])
    landed(pk_in.at[pl.ds(0, 3)], ps.at[0])
    landed(pk_rows.at[pl.ds(0, 3)], qs.at[0])
    landed(hid.at[pl.ds(0, 3)], hs.at[0])
    landed(part_b.at[pl.ds(0, 3)], bs.at[0])


def finish(
    a_gate, a_up, wg_acc, late_rows, late_hid, scales, router, gate_out, up_out, wg_out, router_out,
    gate_v, up_v, wg_v, sem,
):
    local(router, router_out, sem.at[3]).start()

    def write(source, target, part, k):
        local(source.at[part], target.at[part], sem.at[k]).start()

    slots, features = a_gate.shape[0], wg_acc.shape[0]
    step = 128
    for at in range(0, features, step):
        wg_v[at:at + step, :] = (
            wg_acc[at:at + step, :] + lax.dot_general(
                late_rows[:, at:at + step], late_hid[...], (((0,), (0,)), ((), ())),
                preferred_element_type=F32,
            )
        ).astype(BF16)
        write(wg_v, wg_out, pl.ds(at, step), 2)
    size = slots // 4
    for at in range(0, slots, size):
        for k, delta, staged, out in ((0, a_gate, gate_v, gate_out), (1, a_up, up_v, up_out)):
            factor = scales[4 * k:4 * k + 1, 0:1]

            @pl.loop(0, size // 32)
            def _(j):
                part = pl.ds(pl.multiple_of(at + j * 32, 32), 32)
                staged[part, :] = (delta[part, :] * factor).astype(BF16)

            write(staged, out, pl.ds(at, size), k)
    for k, out in enumerate((gate_out, up_out, wg_out, router_out)):
        landed(out, sem.at[k])


def shards(out_grad, router_probs, expert_ids, saved_gate, saved_up, down_weight):
    tok, top = expert_ids.shape
    experts = lax.axis_size("expert")
    cap = saved_gate.shape[3]
    width = saved_gate.shape[4]
    slots = saved_gate.shape[2] * cap
    features = down_weight.shape[1]
    half = slots // 2
    chips = experts // 2
    any_space = pl.BlockSpec(memory_space=pl.ANY)
    hbm = pl.BlockSpec(memory_space=pltpu.HBM)
    vmem = pl.BlockSpec(memory_space=pltpu.VMEM)
    dma = pltpu.SemaphoreType.DMA
    stay = functools.partial(pltpu.with_memory_space_constraint, memory_space=pltpu.HBM)
    shapes = (
        ((slots, width), BF16), ((slots, width), BF16), ((features, width), BF16),
        ((top, tok), F32),
    )
    last = half // 3
    between = (
        ((slots, width), F32), ((slots, width), F32), ((features, width), F32),
        ((last, features), BF16), ((last, width), BF16), ((8, 128), F32), ((top, tok), F32),
    )
    results = pl.pallas_call(
        functools.partial(kernel, experts, cap, tok, top),
        out_shape=tuple(pltpu.VMEM(*shape) for shape in between),
        in_specs=[hbm] * 6,
        out_specs=(vmem,) * len(between),
        scratch_shapes=[
            pltpu.VMEM((top, tok), jnp.int32),
            pltpu.VMEM((top, tok), BF16),
            pltpu.VMEM((2, tok, features // 2), BF16),
            pltpu.VMEM((slots, width), BF16),
            pltpu.VMEM((slots, width), BF16),
            pltpu.VMEM((features, width), BF16),
            pltpu.VMEM((RING, slots, width), BF16),
            pltpu.VMEM((RING, slots, features), BF16),
            pltpu.VMEM((2, tok, features // 2), BF16),
            pltpu.VMEM((8, 128), F32),
            pltpu.VMEM((2, 8, 128), F32),
            pltpu.VMEM((2 * cap * experts, features // 2), BF16),
            pltpu.VMEM((RING, 2, half, width), F32),
            pltpu.VMEM((RING, 2, half, width), BF16),
            pltpu.VMEM((2, half, width), BF16),
            pltpu.VMEM((2, half, width), BF16),
            pltpu.VMEM((2, half, width), BF16),
            pltpu.VMEM((2, half, width), BF16),
            pltpu.VMEM((8, 128), F32),
            pltpu.VMEM((RING, 8, 128), F32),
            pltpu.VMEM((8, 128), F32),
            pltpu.VMEM((RING, 8, 128), F32),
            pltpu.VMEM((slots + 128, 128), F32),
            pltpu.VMEM((1, slots + 128), F32),
            pltpu.VMEM((experts, 1, slots + 128), F32),
            pltpu.VMEM((experts, 128), F32),
            pltpu.VMEM((RING, experts, 128), F32),
            dma((10,)),
            dma((2,)), dma((2,)), dma((2,)), dma((2,)),
            dma((1,)), dma((chips,)),
            dma((1,)), dma((chips + 1,)),
            dma((1,)), dma((6,)),
            dma((1,)), dma((5,)),
            dma((1,)), dma((1,)), dma((1,)), dma((1,)),
            dma((1,)), dma((1,)),
            dma((1,)), dma((1,)),
        ],
        compiler_params=pltpu.CompilerParams(
            collective_id=0, has_side_effects=True, vmem_limit_bytes=40 * 1024 * 1024
        ),
        cost_estimate=pl.CostEstimate(
            flops=4 * RING * slots * features * width,
            bytes_accessed=4 * slots * width + 2 * features * width,
            transcendentals=slots * width,
        ),
    )(
        stay(out_grad), stay(expert_ids.T), stay(router_probs.T), stay(saved_gate.reshape(slots, width)),
        stay(saved_up.reshape(slots, width)), stay(down_weight.reshape(features, width)),
    )
    gate_grad, up_grad, weight_grad, router_grad = pl.pallas_call(
        finish,
        out_shape=tuple(jax.ShapeDtypeStruct(*shape) for shape in shapes),
        in_specs=[vmem] * len(between),
        out_specs=(any_space,) * 4,
        scratch_shapes=[pltpu.VMEM(*shape) for shape in shapes[:3]] + [dma((4,))],
        compiler_params=pltpu.CompilerParams(vmem_limit_bytes=8 * 1024 * 1024),
    )(*(pltpu.with_memory_space_constraint(r, memory_space=pltpu.VMEM) for r in results))
    return (
        gate_grad.reshape(saved_gate.shape), up_grad.reshape(saved_up.shape),
        weight_grad.reshape(down_weight.shape), router_grad.T,
    )


def solution(mesh):
    in_specs = (
        P(("expert", "edata"), None),
        P(("expert", "edata"), None),
        P(("expert", "edata"), None),
        P("expert", "edata", None, None, "tensor"),
        P("expert", "edata", None, None, "tensor"),
        P("expert", "edata", "tensor"),
    )
    out_specs = (
        P("expert", "edata", None, None, "tensor"),
        P("expert", "edata", None, None, "tensor"),
        P("expert", "edata", "tensor"),
        P(("expert", "edata"), None),
    )
    return jax.shard_map(shards, mesh=mesh, in_specs=in_specs, out_specs=out_specs, check_vma=False)
```

```python
import functools

import jax
import jax.numpy as jnp
from jax import lax
from jax.experimental import pallas as pl
from jax.experimental.pallas import tpu as pltpu
from jax.sharding import PartitionSpec as P

MESH = pl.DeviceIdType.MESH
RING = 4
F32 = jnp.float32
BF16 = jnp.bfloat16


def local(src, dst, sem):
    return pltpu.make_async_copy(src, dst, sem)


def landed(ref, sem):
    pltpu.make_async_copy(ref, ref, sem).wait()


def silu_factors(gate_value, up_value):
    sigmoid_gate = jax.nn.sigmoid(gate_value)
    activated = gate_value * sigmoid_gate
    gate_factor = up_value * sigmoid_gate * (1.0 + gate_value * (1.0 - sigmoid_gate))
    return activated * up_value, gate_factor, activated


def kernel(
    experts, cap, tok, top,
    og, ids, probs, gate, up, w,
    a_gate, a_up, wg_acc, late_rows, late_hid, scales, router_out,
    ids_ref, probs_ref, og_v, gate_v, up_v, w_v, hid, rows, x2, meta_own, meta_in, sb,
    part_f, part_b, sb_c, rb_o, rb_d, rb_c,
    pk_own, pk_in, pk_row, pk_rows, rl, rz_out, rz_in, ry_own, ry_in,
    load_sem, xs, xr, ms, mr, zs, zr, ys, yr, hs, hr, bs, br, ps, pr, qs, qr, ws, wr, vs, vr,
):
    e, x, y = lax.axis_index("expert"), lax.axis_index("edata"), lax.axis_index("tensor")
    z, c = lax.div(e, 2), lax.rem(e, 2)
    slots, width = gate.shape
    half = slots // 2
    quarter = half // 2
    features = w.shape[0]
    lanes_half = features // 2
    pair = 2 * cap
    x_right, x_left, x_far = lax.rem(x + 1, RING), lax.rem(x + 3, RING), lax.rem(x + 2, RING)
    y_right, y_left, y_far = lax.rem(y + 1, RING), lax.rem(y + 3, RING), lax.rem(y + 2, RING)
    first, second = pl.ds(0, half), pl.ds(half, half)
    fill_right = x == y
    fill_left = x == y

    def share(core):
        return lax.rem(y - x + 2 * core + RING, RING)

    from_y = lax.rem(x + y + 2 * c, RING)
    gives_home = jnp.logical_and(share(1 - c) == x, x == y)
    takes_home = jnp.logical_and(from_y == y, x == y)
    stays = jnp.logical_and(share(c) == x, x == y)
    gives_near = jnp.logical_or(share(c) == x, x == y)
    takes_near = jnp.logical_or(from_y == y, x == y)

    barrier = pltpu.get_barrier_semaphore()

    def greet(device):
        pl.semaphore_signal(barrier, inc=1, device_id=device, device_id_type=MESH)

    @pl.loop(1, experts)
    def _(i):
        greet((lax.rem(e + i, experts), x, y))

    for i in range(1, RING):
        greet((e, lax.rem(x + i, RING), y))
        greet((e, x, lax.rem(y + i, RING)))

    @pl.when(jnp.logical_not(gives_near))
    def _():
        greet((e, share(c), x))

    @pl.when(jnp.logical_not(takes_near))
    def _():
        greet((e, y, from_y))

    @pl.when(jnp.logical_not(gives_home))
    def _():
        greet((2 * z + 1 - c, share(1 - c), x))

    @pl.when(jnp.logical_not(takes_home))
    def _():
        greet((2 * z + 1 - c, y, from_y))

    loads = [
        tuple(
            local(ref.at[part], held.at[part], load_sem.at[6 + 2 * i + k])
            for k, (ref, held) in enumerate(((gate, gate_v), (up, up_v)))
        )
        for i, part in enumerate((first, second))
    ]
    load_w = local(w, w_v, load_sem.at[2])
    small = (
        local(ids, ids_ref, load_sem.at[3]),
        local(probs, probs_ref, load_sem.at[4]),
    )
    tokens = tuple(
        local(
            og.at[:, pl.ds(
                pl.multiple_of(features * share(core) + lanes_half * core, 128), lanes_half
            )],
            og_v.at[core], load_sem.at[5],
        )
        for core in range(2)
    )
    for copy in small + tokens:
        copy.start()
    for copy in loads[0] + loads[1]:
        copy.start()
    load_w.start()

    place = (
        lax.broadcasted_iota(jnp.int32, (tok, 128), 1)
        == lax.broadcasted_iota(jnp.int32, (tok, 128), 0) + tok * c
    ).astype(F32).astype(BF16)
    for copy in small:
        copy.wait()
    meta_own[0:top, :] = jnp.dot(
        ids_ref[...].astype(F32).astype(BF16), place, preferred_element_type=F32
    )
    meta_own[4:4 + top, :] = jnp.dot(probs_ref[...], place, preferred_element_type=F32)

    def hidden_of(i):
        for copy in loads[i]:
            copy.wait()

        @pl.loop(0, half // 32)
        def _(j):
            part = pl.ds(pl.multiple_of(i * half + j * 32, 32), 32)
            for at in range(0, width, 128):
                lanes = slice(at, at + 128)
                hidden, gate_factor, up_factor = silu_factors(
                    gate_v[part, lanes].astype(F32), up_v[part, lanes].astype(F32)
                )
                hid[x, part, lanes] = hidden.astype(BF16)
                a_gate[part, lanes] = gate_factor
                a_up[part, lanes] = up_factor

    landed(og_v, load_sem.at[5])
    hidden_of(0)
    peers = experts - 1 + 2 * (RING - 1)
    for near in (gives_near, takes_near, gives_home, takes_home):
        peers = peers + jnp.where(near, 0, 1)
    pl.semaphore_wait(barrier, peers)

    def swap(core):
        device = (2 * z + core, share(core), x)
        return (
            pltpu.make_async_remote_copy(
                src_ref=meta_own, dst_ref=meta_in.at[c], send_sem=ms.at[core],
                recv_sem=mr.at[c], device_id=device, device_id_type=MESH,
            ),
            pltpu.make_async_remote_copy(
                src_ref=og_v.at[core], dst_ref=x2.at[c], send_sem=xs.at[core],
                recv_sem=xr.at[c], device_id=device, device_id_type=MESH,
            ),
        )

    for core in range(2):
        at_home = jnp.logical_and(stays, c == core)

        @pl.when(at_home)
        def _():
            local(meta_own, meta_in.at[c], mr.at[c]).start()
            local(og_v.at[core], x2.at[c], xr.at[c]).start()

        @pl.when(jnp.logical_not(at_home))
        def _():
            for copy in swap(core):
                copy.start()

    part_a, part_e = pl.ds(0, quarter), pl.ds(quarter, quarter)
    last = quarter // 3
    more = quarter - last
    part_c, part_d = pl.ds(quarter, more), pl.ds(quarter + more, last)
    far_a = pl.ds(half, quarter)
    far_c, far_d = pl.ds(half + quarter, more), pl.ds(half + quarter + more, last)

    def pass_hidden(index, block, part, to_right):
        at = hid.at[block, part]
        return pltpu.make_async_remote_copy(
            src_ref=at, dst_ref=at, send_sem=hs.at[0], recv_sem=hr.at[index],
            device_id=(e, x_right if to_right else x_left, y), device_id_type=MESH,
        )

    h_r0 = pass_hidden(0, x, first, True)
    h_r1 = pass_hidden(2, x, second, True)
    h_l0 = pass_hidden(2, x, first, False)
    h_l1 = pass_hidden(1, x, second, False)
    h_ra = pass_hidden(3, x_left, part_a, True)
    h_la = pass_hidden(3, x_right, far_a, False)
    h_rc = pass_hidden(4, x_left, part_c, True)
    h_lc = pass_hidden(4, x_right, far_c, False)
    h_rd = pass_hidden(5, x_left, part_d, True)
    h_ld = pass_hidden(5, x_right, far_d, False)
    h_r0.start()
    hidden_of(1)
    for copy in (h_l1, h_r1, h_l0):
        copy.start()
    for core in range(2):
        local(meta_own, meta_in.at[core], mr.at[core]).wait()
        local(x2.at[core], x2.at[core], xr.at[core]).wait()
    meta = meta_in[0] + meta_in[1]
    lane = lax.broadcasted_iota(jnp.int32, (experts, 128), 1)
    expert_row = lax.broadcasted_iota(jnp.int32, (experts, 128), 0).astype(F32)
    member = jnp.zeros((experts, 128), F32)
    scale = jnp.zeros((experts, 128), F32)
    for k in range(top):
        named = meta[k:k + 1, :] == expert_row
        member = jnp.where(named, 1.0, member)
        scale = jnp.where(named, meta[4 + k:5 + k, :], scale)
    live = lane < 2 * tok
    member = jnp.where(live, member, 0.0)
    row_i = lax.broadcasted_iota(jnp.int32, (128, 128), 0)
    lane_i = lax.broadcasted_iota(jnp.int32, (128, 128), 1)
    before = jnp.logical_and(row_i < lane_i, jnp.logical_or(row_i >= tok, lane_i < tok))
    earlier = jnp.dot(
        member.astype(BF16), before.astype(F32).astype(BF16), preferred_element_type=F32
    )
    target = jnp.where(
        member > 0.0, earlier + jnp.where(lane >= tok, float(cap), 0.0), -1.0
    )
    slot_row = lax.broadcasted_iota(jnp.int32, (experts, pair, 128), 1).astype(F32)
    pick = jnp.where(slot_row == target[:, None, :], scale[:, None, :], 0.0).astype(BF16)
    sb[...] = jnp.dot(
        pick.reshape(experts * pair, 128)[:, :2 * tok], x2[...].reshape(2 * tok, lanes_half),
        preferred_element_type=F32,
    ).astype(BF16)
    my_rows = pl.ds(pl.multiple_of(pair * z, 16), pair)
    my_lanes = pl.ds(pl.multiple_of(lanes_half * c, 128), lanes_half)

    def dispatch(to):
        return pltpu.make_async_remote_copy(
            src_ref=sb.at[pl.ds(pl.multiple_of(pair * to, 16), pair)],
            dst_ref=rows.at[y, my_rows, my_lanes],
            send_sem=zs.at[0], recv_sem=zr.at[z],
            device_id=(to, x, y), device_id_type=MESH,
        )

    chips = experts // 2

    def chip(j):
        away = lax.div(j + 1, 2)
        return lax.rem(jnp.where(lax.rem(j, 2) == 1, z + away, z - away + chips), chips)

    local(
        sb.at[pl.ds(pl.multiple_of(pair * e, 16), pair)], rows.at[y, my_rows, my_lanes], zr.at[z]
    ).start()
    dispatch(2 * z + 1 - c).start()

    def dispatch_both(j):
        for core in range(2):
            dispatch(2 * chip(j) + core).start()

    @pl.loop(1, chips)
    def _(j):
        dispatch_both(j)

    def pass_rows(j, block, to_right, sem):
        at = rows.at[block, pl.ds(pl.multiple_of(pair * chip(j), 16), pair)]
        return pltpu.make_async_remote_copy(
            src_ref=at, dst_ref=at, send_sem=ys.at[0], recv_sem=yr.at[sem],
            device_id=(e, x, y_right if to_right else y_left), device_id_type=MESH,
        )

    def go_right(j):
        return pass_rows(j, y, True, j)

    def go_left(j):
        return pass_rows(j, y, False, j)

    def on_right(j):
        return pass_rows(j, y_left, True, chips)

    def on_left(j):
        return pass_rows(j, y_right, False, chips)

    def start_own(j):
        landed(
            rows.at[y, pl.ds(pl.multiple_of(pair * chip(j), 16), pair)], zr.at[chip(j)]
        )
        go_right(j).start()
        go_left(j).start()

    def start_on(j):
        landed(rows.at[pl.ds(0, 2), pl.ds(0, pair)], yr.at[j])

        (on_right, on_left)[j % 2](j).start()

    tiles = [(at, min(256, width - at)) for at in range(0, width, 256)]

    def send(index, src, dst, to_right):
        return pltpu.make_async_remote_copy(
            src_ref=src, dst_ref=dst, send_sem=bs.at[0], recv_sem=br.at[index],
            device_id=(e, x_right if to_right else x_left, y), device_id_type=MESH,
        )

    far0 = send(0, part_b.at[2, 0], rb_o.at[0], True)
    far1 = send(1, part_b.at[2, 1], rb_o.at[1], False)
    near0, near1 = (
        [
            send(2, part_b.at[role, 1 - k, part], rb_d.at[k, part], k == 0)
            for part in (part_a, part_e)
        ]
        for k, role in enumerate((1, 3))
    )
    both = [
        (send(3 + i, sb_c.at[0, part], rb_c.at[0, part], True),
         send(3 + i, sb_c.at[1, part], rb_c.at[1, part], False))
        for i, part in enumerate((part_a, part_e))
    ]

    def partial(replica):
        role = lax.rem(replica - x + RING, RING)
        block = rows[replica]
        for at, size in tiles:
            product = jnp.dot(block, w_v[:, at:at + size], preferred_element_type=F32)
            for i in range(2):
                value = product[i * half:(i + 1) * half]
                part_f[role, i, :, at:at + size] = value
                part_b[role, i, :, at:at + size] = value.astype(BF16)

        @pl.when(role == 2)
        def _():
            far0.start()
            far1.start()

        @pl.when(role == 1)
        def _():
            near0[0].start()

        @pl.when(role == 3)
        def _():
            near1[0].start()

    for j in range(chips):
        start_own(j)

    @pl.when(fill_right)
    def _():
        h_r0.wait_recv()
        h_rc.start()

    @pl.when(fill_left)
    def _():
        h_l1.wait_recv()
        h_lc.start()

    load_w.wait()
    partial(y)

    for k in range(chips):
        start_on(k)

    partial(jnp.where(x == y_right, y_left, y_right))
    partial(jnp.where(x == y_right, y_right, y_left))

    landed(rows.at[y_far], yr.at[chips])
    partial(y_far)
    near0[1].start()
    near1[1].start()

    @pl.when(jnp.logical_not(fill_right))
    def _():
        h_r0.wait_recv()

    @pl.when(jnp.logical_not(fill_left))
    def _():
        h_l1.wait_recv()

    landed(hid.at[x], hr.at[2])
    step = 256 if features % 256 == 0 else 128

    def outer(block, slot_parts, at):
        left = jnp.concatenate([rows[block, p, at:at + step] for p in slot_parts], axis=0)
        right = jnp.concatenate([hid[block, p, :] for p in slot_parts], axis=0)
        return lax.dot_general(
            left, right, (((0,), (0,)), ((), ())), preferred_element_type=F32
        )

    everything = (slice(0, slots),)
    for at in range(0, features, step):
        wg_acc[at:at + step, :] = (
            outer(x, everything, at) + outer(x_left, everything, at) + outer(x_right, everything, at)
        )
    early = (slice(0, quarter), slice(half, half + quarter))
    late = tuple(slice(at, at + more) for at in (quarter, half + quarter))
    latest = tuple(slice(at + more, at + quarter) for at in (quarter, half + quarter))

    for core in range(2):
        @pl.when(jnp.logical_not(jnp.logical_and(stays, c == core)))
        def _():
            for copy in swap(core):
                copy.wait_send()

    landed(sb.at[pl.ds(0, pair * (experts - 1))], zs.at[0])
    landed(rows.at[pl.ds(0, 3)], ys.at[0])

    def pass_on(side):
        @pl.when(side == 0)
        def _():
            far0.wait_recv()

        @pl.when(side == 1)
        def _():
            far1.wait_recv()

        for i in range(2):
            @pl.loop(0, quarter // 16)
            def _(j):
                part = pl.ds(pl.multiple_of(i * quarter + j * 16, 16), 16)
                sb_c[side, part, :] = (
                    part_f[1 + 2 * side, side, part, :] + rb_o[side, part, :].astype(F32)
                ).astype(BF16)

            for k in range(2):
                @pl.when(side == k)
                def _():
                    both[i][k].start()

    early_side = jnp.where(x_left == y, 1, 0)
    pass_on(early_side)
    pass_on(1 - early_side)

    h_ra.start()
    h_la.start()

    @pl.when(jnp.logical_not(fill_right))
    def _():
        h_rc.start()

    @pl.when(jnp.logical_not(fill_left))
    def _():
        h_lc.start()

    landed(rb_d, br.at[2])

    zero = jnp.zeros((16, 128), F32)
    peaks = (zero, zero)
    for i in range(2):
        landed(rb_c.at[pl.ds(0, 2), pl.ds(0, quarter)], br.at[3 + i])
        for side in range(2):
            def body(j, carry):
                gate_peak, up_peak = carry
                part = pl.ds(pl.multiple_of(i * quarter + j * 16, 16), 16)
                at = pl.ds(pl.multiple_of(side * half + i * quarter + j * 16, 16), 16)
                sent = rb_d[1 - side, part, :].astype(F32) + rb_c[side, part, :].astype(F32)
                d_hidden = part_f[0, side, part, :] + sent
                gate_delta = d_hidden * a_gate[at, :]
                up_delta = d_hidden * a_up[at, :]
                a_gate[at, :] = gate_delta
                a_up[at, :] = up_delta
                weighted = up_delta * up_v[at, :].astype(F32)
                total = zero
                for lane0 in range(0, width, 128):
                    sl = slice(lane0, lane0 + 128)
                    gate_peak = jnp.maximum(gate_peak, jnp.abs(gate_delta[:, sl]))
                    up_peak = jnp.maximum(up_peak, jnp.abs(up_delta[:, sl]))
                    total = total + weighted[:, sl]
                rl[at, :] = total
                return gate_peak, up_peak

            peaks = lax.fori_loop(0, quarter // 16, body, peaks)
    peak_row = lax.broadcasted_iota(jnp.int32, (8, 128), 0)
    pk_own[...] = jnp.where(
        peak_row < 4,
        jnp.max(peaks[0], axis=0, keepdims=True), jnp.max(peaks[1], axis=0, keepdims=True),
    )

    def tell_row(p):
        return pltpu.make_async_remote_copy(
            src_ref=pk_own, dst_ref=pk_in.at[y], send_sem=ps.at[0], recv_sem=pr.at[0],
            device_id=(e, x, p), device_id_type=MESH,
        )

    def tell_column(p):
        return pltpu.make_async_remote_copy(
            src_ref=pk_row, dst_ref=pk_rows.at[x], send_sem=qs.at[0], recv_sem=qr.at[0],
            device_id=(e, p, y), device_id_type=MESH,
        )

    y_others, x_others = (y_right, y_left, y_far), (x_right, x_left, x_far)
    for p in y_others:
        tell_row(p).start()

    rl[slots:, :] = jnp.zeros((rl.shape[0] - slots, 128), F32)
    ones = jnp.ones((8, 128), BF16)
    across = (((1,), (1,)), ((), ()))

    def split(value):
        high = value.astype(BF16)
        return high, (value - high.astype(F32)).astype(BF16)

    sums = sum(
        lax.dot_general(ones, part, across, preferred_element_type=F32) for part in split(rl[...])
    )
    rz_out[...] = sums[0:1, :]

    def give_back(to):
        return pltpu.make_async_remote_copy(
            src_ref=rz_out, dst_ref=rz_in.at[e], send_sem=ws.at[0], recv_sem=wr.at[0],
            device_id=(to, x, y), device_id_type=MESH,
        )

    @pl.loop(1, experts)
    def _(i):
        give_back(lax.rem(e + i, experts)).start()

    rz_in[e] = rz_out[...]
    row_peak = pk_own[...]
    landed(pk_in.at[pl.ds(0, 3)], pr.at[0])
    for p in y_others:
        row_peak = jnp.maximum(row_peak, pk_in[p])
    pk_row[...] = row_peak
    for p in x_others:
        tell_column(p).start()
    h_rd.start()
    h_ld.start()
    landed(rz_in.at[pl.ds(0, experts - 1)], wr.at[0])
    from_experts = rz_in[:, 0, :]
    mine = (
        lax.broadcasted_iota(jnp.int32, (128, from_experts.shape[1]), 1)
        == lax.broadcasted_iota(jnp.int32, (128, from_experts.shape[1]), 0) + cap * e
    ).astype(F32).astype(BF16)
    ry_own[...] = sum(
        lax.dot_general(part, mine, across, preferred_element_type=F32)
        for part in split(from_experts)
    )

    def tell_sum(p):
        return pltpu.make_async_remote_copy(
            src_ref=ry_own, dst_ref=ry_in.at[y], send_sem=vs.at[0], recv_sem=vr.at[0],
            device_id=(e, x, p), device_id_type=MESH,
        )

    for p in y_others:
        tell_sum(p).start()

    landed(hid.at[x_far, pl.ds(0, 2 * quarter)], hr.at[3])
    for at in range(0, features, step):
        wg_acc[at:at + step, :] += outer(x_far, early, at)

    all_peaks = row_peak
    landed(pk_rows.at[pl.ds(0, 3)], qr.at[0])
    for p in x_others:
        all_peaks = jnp.maximum(all_peaks, pk_rows[p])
    scales[...] = 1.0 / (
        jnp.where(
            peak_row < 4,
            jnp.max(all_peaks[:4], axis=(0, 1), keepdims=True),
            jnp.max(all_peaks[4:], axis=(0, 1), keepdims=True),
        ) + 1e-6
    )
    landed(hid.at[x_far, pl.ds(0, 2 * more)], hr.at[4])
    for at in range(0, features, step):
        wg_acc[at:at + step, :] += outer(x_far, late, at)

    ids_f = ids_ref[...].astype(F32)
    expert_col = lax.broadcasted_iota(jnp.int32, (experts, tok), 0).astype(F32)
    named = [(ids_f[k:k + 1, :] == expert_col).astype(F32) for k in range(top)]
    tri = (
        lax.broadcasted_iota(jnp.int32, (tok, tok), 0)
        < lax.broadcasted_iota(jnp.int32, (tok, tok), 1)
    ).astype(F32).astype(BF16)
    earlier = jnp.dot(sum(named).astype(BF16), tri, preferred_element_type=F32)
    slot_col = lax.broadcasted_iota(jnp.int32, (128, tok), 0).astype(F32)
    at_slot = [
        slot_col == jnp.sum(earlier * named[k], axis=0, keepdims=True) for k in range(top)
    ]
    landed(ry_in.at[pl.ds(0, 3)], vr.at[0])
    sums = ry_own[...]
    for p in y_others:
        sums = sums + ry_in[p]
    high, low = split(sums)
    down = (((0,), (0,)), ((), ()))
    for k in range(top):
        pick = named[k].astype(BF16)
        found = lax.dot_general(
            high, pick, down, preferred_element_type=F32
        ) + lax.dot_general(low, pick, down, preferred_element_type=F32)
        value = jnp.sum(jnp.where(at_slot[k], found, 0.0), axis=0, keepdims=True)
        router_out[k:k + 1, :] = value / probs_ref[k:k + 1, :].astype(F32)

    landed(hid.at[x_far, pl.ds(0, 2 * last)], hr.at[5])
    late_rows[...] = jnp.concatenate([rows[x_far, p, :] for p in latest], axis=0)
    late_hid[...] = jnp.concatenate([hid[x_far, p, :] for p in latest], axis=0)

    landed(rz_in.at[pl.ds(0, experts - 1)], ws.at[0])
    landed(ry_in.at[pl.ds(0, 3)], vs.at[0])
    landed(pk_in.at[pl.ds(0, 3)], ps.at[0])
    landed(pk_rows.at[pl.ds(0, 3)], qs.at[0])
    landed(hid.at[pl.ds(0, 3)], hs.at[0])
    landed(part_b.at[pl.ds(0, 3)], bs.at[0])


def finish(
    a_gate, a_up, wg_acc, late_rows, late_hid, scales, router, gate_out, up_out, wg_out, router_out,
    gate_v, up_v, wg_v, sem,
):
    local(router, router_out, sem.at[3]).start()

    def write(source, target, part, k):
        local(source.at[part], target.at[part], sem.at[k]).start()

    slots, features = a_gate.shape[0], wg_acc.shape[0]
    step = 128
    for at in range(0, features, step):
        wg_v[at:at + step, :] = (
            wg_acc[at:at + step, :] + lax.dot_general(
                late_rows[:, at:at + step], late_hid[...], (((0,), (0,)), ((), ())),
                preferred_element_type=F32,
            )
        ).astype(BF16)
        write(wg_v, wg_out, pl.ds(at, step), 2)
    size = slots // 4
    for at in range(0, slots, size):
        for k, delta, staged, out in ((0, a_gate, gate_v, gate_out), (1, a_up, up_v, up_out)):
            factor = scales[4 * k:4 * k + 1, 0:1]

            @pl.loop(0, size // 32)
            def _(j):
                part = pl.ds(pl.multiple_of(at + j * 32, 32), 32)
                staged[part, :] = (delta[part, :] * factor).astype(BF16)

            write(staged, out, pl.ds(at, size), k)
    for k, out in enumerate((gate_out, up_out, wg_out, router_out)):
        landed(out, sem.at[k])


def shards(out_grad, router_probs, expert_ids, saved_gate, saved_up, down_weight):
    tok, top = expert_ids.shape
    experts = lax.axis_size("expert")
    cap = saved_gate.shape[3]
    width = saved_gate.shape[4]
    slots = saved_gate.shape[2] * cap
    features = down_weight.shape[1]
    half = slots // 2
    chips = experts // 2
    any_space = pl.BlockSpec(memory_space=pl.ANY)
    hbm = pl.BlockSpec(memory_space=pltpu.HBM)
    vmem = pl.BlockSpec(memory_space=pltpu.VMEM)
    dma = pltpu.SemaphoreType.DMA
    stay = functools.partial(pltpu.with_memory_space_constraint, memory_space=pltpu.HBM)
    shapes = (
        ((slots, width), BF16), ((slots, width), BF16), ((features, width), BF16),
        ((top, tok), F32),
    )
    last = half // 3
    between = (
        ((slots, width), F32), ((slots, width), F32), ((features, width), F32),
        ((last, features), BF16), ((last, width), BF16), ((8, 128), F32), ((top, tok), F32),
    )
    results = pl.pallas_call(
        functools.partial(kernel, experts, cap, tok, top),
        out_shape=tuple(pltpu.VMEM(*shape) for shape in between),
        in_specs=[hbm] * 6,
        out_specs=(vmem,) * len(between),
        scratch_shapes=[
            pltpu.VMEM((top, tok), jnp.int32),
            pltpu.VMEM((top, tok), BF16),
            pltpu.VMEM((2, tok, features // 2), BF16),
            pltpu.VMEM((slots, width), BF16),
            pltpu.VMEM((slots, width), BF16),
            pltpu.VMEM((features, width), BF16),
            pltpu.VMEM((RING, slots, width), BF16),
            pltpu.VMEM((RING, slots, features), BF16),
            pltpu.VMEM((2, tok, features // 2), BF16),
            pltpu.VMEM((8, 128), F32),
            pltpu.VMEM((2, 8, 128), F32),
            pltpu.VMEM((2 * cap * experts, features // 2), BF16),
            pltpu.VMEM((RING, 2, half, width), F32),
            pltpu.VMEM((RING, 2, half, width), BF16),
            pltpu.VMEM((2, half, width), BF16),
            pltpu.VMEM((2, half, width), BF16),
            pltpu.VMEM((2, half, width), BF16),
            pltpu.VMEM((2, half, width), BF16),
            pltpu.VMEM((8, 128), F32),
            pltpu.VMEM((RING, 8, 128), F32),
            pltpu.VMEM((8, 128), F32),
            pltpu.VMEM((RING, 8, 128), F32),
            pltpu.VMEM((slots + 128, 128), F32),
            pltpu.VMEM((1, slots + 128), F32),
            pltpu.VMEM((experts, 1, slots + 128), F32),
            pltpu.VMEM((experts, 128), F32),
            pltpu.VMEM((RING, experts, 128), F32),
            dma((10,)),
            dma((2,)), dma((2,)), dma((2,)), dma((2,)),
            dma((1,)), dma((chips,)),
            dma((1,)), dma((chips + 1,)),
            dma((1,)), dma((6,)),
            dma((1,)), dma((5,)),
            dma((1,)), dma((1,)), dma((1,)), dma((1,)),
            dma((1,)), dma((1,)),
            dma((1,)), dma((1,)),
        ],
        compiler_params=pltpu.CompilerParams(
            collective_id=0, has_side_effects=True, vmem_limit_bytes=40 * 1024 * 1024
        ),
        cost_estimate=pl.CostEstimate(
            flops=4 * RING * slots * features * width,
            bytes_accessed=4 * slots * width + 2 * features * width,
            transcendentals=slots * width,
        ),
    )(
        stay(out_grad), stay(expert_ids.T), stay(router_probs.T), stay(saved_gate.reshape(slots, width)),
        stay(saved_up.reshape(slots, width)), stay(down_weight.reshape(features, width)),
    )
    gate_grad, up_grad, weight_grad, router_grad = pl.pallas_call(
        finish,
        out_shape=tuple(jax.ShapeDtypeStruct(*shape) for shape in shapes),
        in_specs=[vmem] * len(between),
        out_specs=(any_space,) * 4,
        scratch_shapes=[pltpu.VMEM(*shape) for shape in shapes[:3]] + [dma((4,))],
        compiler_params=pltpu.CompilerParams(vmem_limit_bytes=8 * 1024 * 1024),
    )(*(pltpu.with_memory_space_constraint(r, memory_space=pltpu.VMEM) for r in results))
    return (
        gate_grad.reshape(saved_gate.shape), up_grad.reshape(saved_up.shape),
        weight_grad.reshape(down_weight.shape), router_grad.T,
    )


def solution(mesh):
    in_specs = (
        P(("expert", "edata"), None),
        P(("expert", "edata"), None),
        P(("expert", "edata"), None),
        P("expert", "edata", None, None, "tensor"),
        P("expert", "edata", None, None, "tensor"),
        P("expert", "edata", "tensor"),
    )
    out_specs = (
        P("expert", "edata", None, None, "tensor"),
        P("expert", "edata", None, None, "tensor"),
        P("expert", "edata", "tensor"),
        P(("expert", "edata"), None),
    )
    return jax.shard_map(shards, mesh=mesh, in_specs=in_specs, out_specs=out_specs, check_vma=False)
```

```python
import functools

import jax
import jax.numpy as jnp
from jax import lax
from jax.experimental import pallas as pl
from jax.experimental.pallas import tpu as pltpu
from jax.sharding import PartitionSpec as P

MESH = pl.DeviceIdType.MESH
RING = 4
F32 = jnp.float32
BF16 = jnp.bfloat16


def local(src, dst, sem):
    return pltpu.make_async_copy(src, dst, sem)


def landed(ref, sem):
    pltpu.make_async_copy(ref, ref, sem).wait()


def silu_factors(gate_value, up_value):
    sigmoid_gate = jax.nn.sigmoid(gate_value)
    activated = gate_value * sigmoid_gate
    gate_factor = up_value * sigmoid_gate * (1.0 + gate_value * (1.0 - sigmoid_gate))
    return activated * up_value, gate_factor, activated


def kernel(
    experts, cap, tok, top,
    og, ids, probs, gate, up, w,
    a_gate, a_up, wg_acc, late_rows, late_hid, scales, router_out,
    ids_ref, probs_ref, og_v, gate_v, up_v, w_v, hid, rows, x2, meta_own, meta_in, sb,
    part_f, part_b, sb_c, rb_o, rb_d, rb_c,
    pk_own, pk_in, pk_row, pk_rows, rl, rz_out, rz_in, ry_own, ry_in,
    load_sem, xs, xr, ms, mr, zs, zr, ys, yr, hs, hr, bs, br, ps, pr, qs, qr, ws, wr, vs, vr,
):
    e, x, y = lax.axis_index("expert"), lax.axis_index("edata"), lax.axis_index("tensor")
    z, c = lax.div(e, 2), lax.rem(e, 2)
    slots, width = gate.shape
    half = slots // 2
    quarter = half // 2
    features = w.shape[0]
    lanes_half = features // 2
    pair = 2 * cap
    x_right, x_left, x_far = lax.rem(x + 1, RING), lax.rem(x + 3, RING), lax.rem(x + 2, RING)
    y_right, y_left, y_far = lax.rem(y + 1, RING), lax.rem(y + 3, RING), lax.rem(y + 2, RING)
    first, second = pl.ds(0, half), pl.ds(half, half)
    fill_right = x == y
    fill_left = x == y

    def share(core):
        return lax.rem(y - x + 2 * core + RING, RING)

    from_y = lax.rem(x + y + 2 * c, RING)
    gives_home = jnp.logical_and(share(1 - c) == x, x == y)
    takes_home = jnp.logical_and(from_y == y, x == y)
    stays = jnp.logical_and(share(c) == x, x == y)
    gives_near = jnp.logical_or(share(c) == x, x == y)
    takes_near = jnp.logical_or(from_y == y, x == y)

    barrier = pltpu.get_barrier_semaphore()

    def greet(device):
        pl.semaphore_signal(barrier, inc=1, device_id=device, device_id_type=MESH)

    @pl.loop(1, experts)
    def _(i):
        greet((lax.rem(e + i, experts), x, y))

    for i in range(1, RING):
        greet((e, lax.rem(x + i, RING), y))
        greet((e, x, lax.rem(y + i, RING)))

    @pl.when(jnp.logical_not(gives_near))
    def _():
        greet((e, share(c), x))

    @pl.when(jnp.logical_not(takes_near))
    def _():
        greet((e, y, from_y))

    @pl.when(jnp.logical_not(gives_home))
    def _():
        greet((2 * z + 1 - c, share(1 - c), x))

    @pl.when(jnp.logical_not(takes_home))
    def _():
        greet((2 * z + 1 - c, y, from_y))

    loads = [
        tuple(
            local(ref.at[part], held.at[part], load_sem.at[6 + 2 * i + k])
            for k, (ref, held) in enumerate(((gate, gate_v), (up, up_v)))
        )
        for i, part in enumerate((first, second))
    ]
    load_w = local(w, w_v, load_sem.at[2])
    small = (
        local(ids, ids_ref, load_sem.at[3]),
        local(probs, probs_ref, load_sem.at[4]),
    )
    tokens = tuple(
        local(
            og.at[:, pl.ds(
                pl.multiple_of(features * share(core) + lanes_half * core, 128), lanes_half
            )],
            og_v.at[core], load_sem.at[5],
        )
        for core in range(2)
    )
    for copy in small + tokens:
        copy.start()
    for copy in loads[0] + loads[1]:
        copy.start()
    load_w.start()

    place = (
        lax.broadcasted_iota(jnp.int32, (tok, 128), 1)
        == lax.broadcasted_iota(jnp.int32, (tok, 128), 0) + tok * c
    ).astype(F32).astype(BF16)
    for copy in small:
        copy.wait()
    meta_own[0:top, :] = jnp.dot(
        ids_ref[...].astype(F32).astype(BF16), place, preferred_element_type=F32
    )
    meta_own[4:4 + top, :] = jnp.dot(probs_ref[...], place, preferred_element_type=F32)

    def hidden_of(i):
        for copy in loads[i]:
            copy.wait()

        @pl.loop(0, half // 32)
        def _(j):
            part = pl.ds(pl.multiple_of(i * half + j * 32, 32), 32)
            for at in range(0, width, 128):
                lanes = slice(at, at + 128)
                hidden, gate_factor, up_factor = silu_factors(
                    gate_v[part, lanes].astype(F32), up_v[part, lanes].astype(F32)
                )
                hid[x, part, lanes] = hidden.astype(BF16)
                a_gate[part, lanes] = gate_factor
                a_up[part, lanes] = up_factor

    landed(og_v, load_sem.at[5])
    hidden_of(0)
    peers = experts - 1 + 2 * (RING - 1)
    for near in (gives_near, takes_near, gives_home, takes_home):
        peers = peers + jnp.where(near, 0, 1)
    pl.semaphore_wait(barrier, peers)

    def swap(core):
        device = (2 * z + core, share(core), x)
        return (
            pltpu.make_async_remote_copy(
                src_ref=meta_own, dst_ref=meta_in.at[c], send_sem=ms.at[core],
                recv_sem=mr.at[c], device_id=device, device_id_type=MESH,
            ),
            pltpu.make_async_remote_copy(
                src_ref=og_v.at[core], dst_ref=x2.at[c], send_sem=xs.at[core],
                recv_sem=xr.at[c], device_id=device, device_id_type=MESH,
            ),
        )

    for core in range(2):
        at_home = jnp.logical_and(stays, c == core)

        @pl.when(at_home)
        def _():
            local(meta_own, meta_in.at[c], mr.at[c]).start()
            local(og_v.at[core], x2.at[c], xr.at[c]).start()

        @pl.when(jnp.logical_not(at_home))
        def _():
            for copy in swap(core):
                copy.start()

    part_a, part_e = pl.ds(0, quarter), pl.ds(quarter, quarter)
    last = quarter // 2
    more = quarter - last
    part_c, part_d = pl.ds(quarter, more), pl.ds(quarter + more, last)
    far_a = pl.ds(half, quarter)
    far_c, far_d = pl.ds(half + quarter, more), pl.ds(half + quarter + more, last)

    def pass_hidden(index, block, part, to_right):
        at = hid.at[block, part]
        return pltpu.make_async_remote_copy(
            src_ref=at, dst_ref=at, send_sem=hs.at[0], recv_sem=hr.at[index],
            device_id=(e, x_right if to_right else x_left, y), device_id_type=MESH,
        )

    h_r0 = pass_hidden(0, x, first, True)
    h_r1 = pass_hidden(2, x, second, True)
    h_l0 = pass_hidden(2, x, first, False)
    h_l1 = pass_hidden(1, x, second, False)
    h_ra = pass_hidden(3, x_left, part_a, True)
    h_la = pass_hidden(3, x_right, far_a, False)
    h_rc = pass_hidden(4, x_left, part_c, True)
    h_lc = pass_hidden(4, x_right, far_c, False)
    h_rd = pass_hidden(5, x_left, part_d, True)
    h_ld = pass_hidden(5, x_right, far_d, False)
    h_r0.start()
    hidden_of(1)
    for copy in (h_l1, h_r1, h_l0):
        copy.start()
    for core in range(2):
        local(meta_own, meta_in.at[core], mr.at[core]).wait()
        local(x2.at[core], x2.at[core], xr.at[core]).wait()
    meta = meta_in[0] + meta_in[1]
    lane = lax.broadcasted_iota(jnp.int32, (experts, 128), 1)
    expert_row = lax.broadcasted_iota(jnp.int32, (experts, 128), 0).astype(F32)
    member = jnp.zeros((experts, 128), F32)
    scale = jnp.zeros((experts, 128), F32)
    for k in range(top):
        named = meta[k:k + 1, :] == expert_row
        member = jnp.where(named, 1.0, member)
        scale = jnp.where(named, meta[4 + k:5 + k, :], scale)
    live = lane < 2 * tok
    member = jnp.where(live, member, 0.0)
    row_i = lax.broadcasted_iota(jnp.int32, (128, 128), 0)
    lane_i = lax.broadcasted_iota(jnp.int32, (128, 128), 1)
    before = jnp.logical_and(row_i < lane_i, jnp.logical_or(row_i >= tok, lane_i < tok))
    earlier = jnp.dot(
        member.astype(BF16), before.astype(F32).astype(BF16), preferred_element_type=F32
    )
    target = jnp.where(
        member > 0.0, earlier + jnp.where(lane >= tok, float(cap), 0.0), -1.0
    )
    slot_row = lax.broadcasted_iota(jnp.int32, (experts, pair, 128), 1).astype(F32)
    pick = jnp.where(slot_row == target[:, None, :], scale[:, None, :], 0.0).astype(BF16)
    sb[...] = jnp.dot(
        pick.reshape(experts * pair, 128)[:, :2 * tok], x2[...].reshape(2 * tok, lanes_half),
        preferred_element_type=F32,
    ).astype(BF16)
    my_rows = pl.ds(pl.multiple_of(pair * z, 16), pair)
    my_lanes = pl.ds(pl.multiple_of(lanes_half * c, 128), lanes_half)

    def dispatch(to):
        return pltpu.make_async_remote_copy(
            src_ref=sb.at[pl.ds(pl.multiple_of(pair * to, 16), pair)],
            dst_ref=rows.at[y, my_rows, my_lanes],
            send_sem=zs.at[0], recv_sem=zr.at[z],
            device_id=(to, x, y), device_id_type=MESH,
        )

    chips = experts // 2

    def chip(j):
        away = lax.div(j + 1, 2)
        return lax.rem(jnp.where(lax.rem(j, 2) == 1, z + away, z - away + chips), chips)

    local(
        sb.at[pl.ds(pl.multiple_of(pair * e, 16), pair)], rows.at[y, my_rows, my_lanes], zr.at[z]
    ).start()
    dispatch(2 * z + 1 - c).start()

    def dispatch_both(j):
        for core in range(2):
            dispatch(2 * chip(j) + core).start()

    @pl.loop(1, chips)
    def _(j):
        dispatch_both(j)

    def pass_rows(j, block, to_right, sem):
        at = rows.at[block, pl.ds(pl.multiple_of(pair * chip(j), 16), pair)]
        return pltpu.make_async_remote_copy(
            src_ref=at, dst_ref=at, send_sem=ys.at[0], recv_sem=yr.at[sem],
            device_id=(e, x, y_right if to_right else y_left), device_id_type=MESH,
        )

    def go_right(j):
        return pass_rows(j, y, True, j)

    def go_left(j):
        return pass_rows(j, y, False, j)

    def on_right(j):
        return pass_rows(j, y_left, True, chips)

    def on_left(j):
        return pass_rows(j, y_right, False, chips)

    def start_own(j):
        landed(
            rows.at[y, pl.ds(pl.multiple_of(pair * chip(j), 16), pair)], zr.at[chip(j)]
        )
        go_right(j).start()
        go_left(j).start()

    def start_on(j):
        landed(rows.at[pl.ds(0, 2), pl.ds(0, pair)], yr.at[j])

        (on_right, on_left)[j % 2](j).start()

    tiles = [(at, min(256, width - at)) for at in range(0, width, 256)]

    def send(index, src, dst, to_right):
        return pltpu.make_async_remote_copy(
            src_ref=src, dst_ref=dst, send_sem=bs.at[0], recv_sem=br.at[index],
            device_id=(e, x_right if to_right else x_left, y), device_id_type=MESH,
        )

    far0 = send(0, part_b.at[2, 0], rb_o.at[0], True)
    far1 = send(1, part_b.at[2, 1], rb_o.at[1], False)
    near0, near1 = (
        [
            send(2, part_b.at[role, 1 - k, part], rb_d.at[k, part], k == 0)
            for part in (part_a, part_e)
        ]
        for k, role in enumerate((1, 3))
    )
    both = [
        (send(3 + i, sb_c.at[0, part], rb_c.at[0, part], True),
         send(3 + i, sb_c.at[1, part], rb_c.at[1, part], False))
        for i, part in enumerate((part_a, part_e))
    ]

    def partial(replica):
        role = lax.rem(replica - x + RING, RING)
        block = rows[replica]
        for at, size in tiles:
            product = jnp.dot(block, w_v[:, at:at + size], preferred_element_type=F32)
            for i in range(2):
                value = product[i * half:(i + 1) * half]
                part_f[role, i, :, at:at + size] = value
                part_b[role, i, :, at:at + size] = value.astype(BF16)

        @pl.when(role == 2)
        def _():
            far0.start()
            far1.start()

        @pl.when(role == 1)
        def _():
            near0[0].start()

        @pl.when(role == 3)
        def _():
            near1[0].start()

    for j in range(chips):
        start_own(j)

    @pl.when(fill_right)
    def _():
        h_r0.wait_recv()
        h_rc.start()

    @pl.when(fill_left)
    def _():
        h_l1.wait_recv()
        h_lc.start()

    load_w.wait()
    partial(y)

    for k in range(chips):
        start_on(k)

    partial(jnp.where(x == y_right, y_left, y_right))
    partial(jnp.where(x == y_right, y_right, y_left))

    landed(rows.at[y_far], yr.at[chips])
    partial(y_far)
    near0[1].start()
    near1[1].start()

    @pl.when(jnp.logical_not(fill_right))
    def _():
        h_r0.wait_recv()

    @pl.when(jnp.logical_not(fill_left))
    def _():
        h_l1.wait_recv()

    landed(hid.at[x], hr.at[2])
    step = 256 if features % 256 == 0 else 128

    def outer(block, slot_parts, at):
        left = jnp.concatenate([rows[block, p, at:at + step] for p in slot_parts], axis=0)
        right = jnp.concatenate([hid[block, p, :] for p in slot_parts], axis=0)
        return lax.dot_general(
            left, right, (((0,), (0,)), ((), ())), preferred_element_type=F32
        )

    everything = (slice(0, slots),)
    for at in range(0, features, step):
        wg_acc[at:at + step, :] = (
            outer(x, everything, at) + outer(x_left, everything, at) + outer(x_right, everything, at)
        )
    early = (slice(0, quarter), slice(half, half + quarter))
    late = tuple(slice(at, at + more) for at in (quarter, half + quarter))
    latest = tuple(slice(at + more, at + quarter) for at in (quarter, half + quarter))

    for core in range(2):
        @pl.when(jnp.logical_not(jnp.logical_and(stays, c == core)))
        def _():
            for copy in swap(core):
                copy.wait_send()

    landed(sb.at[pl.ds(0, pair * (experts - 1))], zs.at[0])
    landed(rows.at[pl.ds(0, 3)], ys.at[0])

    def pass_on(side):
        @pl.when(side == 0)
        def _():
            far0.wait_recv()

        @pl.when(side == 1)
        def _():
            far1.wait_recv()

        for i in range(2):
            @pl.loop(0, quarter // 16)
            def _(j):
                part = pl.ds(pl.multiple_of(i * quarter + j * 16, 16), 16)
                sb_c[side, part, :] = (
                    part_f[1 + 2 * side, side, part, :] + rb_o[side, part, :].astype(F32)
                ).astype(BF16)

            for k in range(2):
                @pl.when(side == k)
                def _():
                    both[i][k].start()

    early_side = jnp.where(x_left == y, 1, 0)
    pass_on(early_side)
    pass_on(1 - early_side)

    h_ra.start()
    h_la.start()

    @pl.when(jnp.logical_not(fill_right))
    def _():
        h_rc.start()

    @pl.when(jnp.logical_not(fill_left))
    def _():
        h_lc.start()

    landed(rb_d, br.at[2])

    zero = jnp.zeros((16, 128), F32)
    peaks = (zero, zero)
    for i in range(2):
        landed(rb_c.at[pl.ds(0, 2), pl.ds(0, quarter)], br.at[3 + i])
        for side in range(2):
            def body(j, carry):
                gate_peak, up_peak = carry
                part = pl.ds(pl.multiple_of(i * quarter + j * 16, 16), 16)
                at = pl.ds(pl.multiple_of(side * half + i * quarter + j * 16, 16), 16)
                sent = rb_d[1 - side, part, :].astype(F32) + rb_c[side, part, :].astype(F32)
                d_hidden = part_f[0, side, part, :] + sent
                gate_delta = d_hidden * a_gate[at, :]
                up_delta = d_hidden * a_up[at, :]
                a_gate[at, :] = gate_delta
                a_up[at, :] = up_delta
                weighted = up_delta * up_v[at, :].astype(F32)
                total = zero
                for lane0 in range(0, width, 128):
                    sl = slice(lane0, lane0 + 128)
                    gate_peak = jnp.maximum(gate_peak, jnp.abs(gate_delta[:, sl]))
                    up_peak = jnp.maximum(up_peak, jnp.abs(up_delta[:, sl]))
                    total = total + weighted[:, sl]
                rl[at, :] = total
                return gate_peak, up_peak

            peaks = lax.fori_loop(0, quarter // 16, body, peaks)
    peak_row = lax.broadcasted_iota(jnp.int32, (8, 128), 0)
    pk_own[...] = jnp.where(
        peak_row < 4,
        jnp.max(peaks[0], axis=0, keepdims=True), jnp.max(peaks[1], axis=0, keepdims=True),
    )

    def tell_row(p):
        return pltpu.make_async_remote_copy(
            src_ref=pk_own, dst_ref=pk_in.at[y], send_sem=ps.at[0], recv_sem=pr.at[0],
            device_id=(e, x, p), device_id_type=MESH,
        )

    def tell_column(p):
        return pltpu.make_async_remote_copy(
            src_ref=pk_row, dst_ref=pk_rows.at[x], send_sem=qs.at[0], recv_sem=qr.at[0],
            device_id=(e, p, y), device_id_type=MESH,
        )

    y_others, x_others = (y_right, y_left, y_far), (x_right, x_left, x_far)
    for p in y_others:
        tell_row(p).start()

    rl[slots:, :] = jnp.zeros((rl.shape[0] - slots, 128), F32)
    ones = jnp.ones((8, 128), BF16)
    across = (((1,), (1,)), ((), ()))

    def split(value):
        high = value.astype(BF16)
        return high, (value - high.astype(F32)).astype(BF16)

    sums = sum(
        lax.dot_general(ones, part, across, preferred_element_type=F32) for part in split(rl[...])
    )
    rz_out[...] = sums[0:1, :]

    def give_back(to):
        return pltpu.make_async_remote_copy(
            src_ref=rz_out, dst_ref=rz_in.at[e], send_sem=ws.at[0], recv_sem=wr.at[0],
            device_id=(to, x, y), device_id_type=MESH,
        )

    @pl.loop(1, experts)
    def _(i):
        give_back(lax.rem(e + i, experts)).start()

    rz_in[e] = rz_out[...]
    row_peak = pk_own[...]
    landed(pk_in.at[pl.ds(0, 3)], pr.at[0])
    for p in y_others:
        row_peak = jnp.maximum(row_peak, pk_in[p])
    pk_row[...] = row_peak
    for p in x_others:
        tell_column(p).start()
    h_rd.start()
    h_ld.start()
    landed(rz_in.at[pl.ds(0, experts - 1)], wr.at[0])
    from_experts = rz_in[:, 0, :]
    mine = (
        lax.broadcasted_iota(jnp.int32, (128, from_experts.shape[1]), 1)
        == lax.broadcasted_iota(jnp.int32, (128, from_experts.shape[1]), 0) + cap * e
    ).astype(F32).astype(BF16)
    ry_own[...] = sum(
        lax.dot_general(part, mine, across, preferred_element_type=F32)
        for part in split(from_experts)
    )

    def tell_sum(p):
        return pltpu.make_async_remote_copy(
            src_ref=ry_own, dst_ref=ry_in.at[y], send_sem=vs.at[0], recv_sem=vr.at[0],
            device_id=(e, x, p), device_id_type=MESH,
        )

    for p in y_others:
        tell_sum(p).start()

    landed(hid.at[x_far, pl.ds(0, 2 * quarter)], hr.at[3])
    for at in range(0, features, step):
        wg_acc[at:at + step, :] += outer(x_far, early, at)

    all_peaks = row_peak
    landed(pk_rows.at[pl.ds(0, 3)], qr.at[0])
    for p in x_others:
        all_peaks = jnp.maximum(all_peaks, pk_rows[p])
    scales[...] = 1.0 / (
        jnp.where(
            peak_row < 4,
            jnp.max(all_peaks[:4], axis=(0, 1), keepdims=True),
            jnp.max(all_peaks[4:], axis=(0, 1), keepdims=True),
        ) + 1e-6
    )
    landed(hid.at[x_far, pl.ds(0, 2 * more)], hr.at[4])
    for at in range(0, features, step):
        wg_acc[at:at + step, :] += outer(x_far, late, at)

    ids_f = ids_ref[...].astype(F32)
    expert_col = lax.broadcasted_iota(jnp.int32, (experts, tok), 0).astype(F32)
    named = [(ids_f[k:k + 1, :] == expert_col).astype(F32) for k in range(top)]
    tri = (
        lax.broadcasted_iota(jnp.int32, (tok, tok), 0)
        < lax.broadcasted_iota(jnp.int32, (tok, tok), 1)
    ).astype(F32).astype(BF16)
    earlier = jnp.dot(sum(named).astype(BF16), tri, preferred_element_type=F32)
    slot_col = lax.broadcasted_iota(jnp.int32, (128, tok), 0).astype(F32)
    at_slot = [
        slot_col == jnp.sum(earlier * named[k], axis=0, keepdims=True) for k in range(top)
    ]
    landed(ry_in.at[pl.ds(0, 3)], vr.at[0])
    sums = ry_own[...]
    for p in y_others:
        sums = sums + ry_in[p]
    high, low = split(sums)
    down = (((0,), (0,)), ((), ()))
    for k in range(top):
        pick = named[k].astype(BF16)
        found = lax.dot_general(
            high, pick, down, preferred_element_type=F32
        ) + lax.dot_general(low, pick, down, preferred_element_type=F32)
        value = jnp.sum(jnp.where(at_slot[k], found, 0.0), axis=0, keepdims=True)
        router_out[k:k + 1, :] = value / probs_ref[k:k + 1, :].astype(F32)

    landed(hid.at[x_far, pl.ds(0, 2 * last)], hr.at[5])
    late_rows[...] = jnp.concatenate([rows[x_far, p, :] for p in latest], axis=0)
    late_hid[...] = jnp.concatenate([hid[x_far, p, :] for p in latest], axis=0)

    landed(rz_in.at[pl.ds(0, experts - 1)], ws.at[0])
    landed(ry_in.at[pl.ds(0, 3)], vs.at[0])
    landed(pk_in.at[pl.ds(0, 3)], ps.at[0])
    landed(pk_rows.at[pl.ds(0, 3)], qs.at[0])
    landed(hid.at[pl.ds(0, 3)], hs.at[0])
    landed(part_b.at[pl.ds(0, 3)], bs.at[0])


def finish(
    a_gate, a_up, wg_acc, late_rows, late_hid, scales, router, gate_out, up_out, wg_out, router_out,
    gate_v, up_v, wg_v, sem,
):
    local(router, router_out, sem.at[3]).start()

    def write(source, target, part, k):
        local(source.at[part], target.at[part], sem.at[k]).start()

    slots, features = a_gate.shape[0], wg_acc.shape[0]
    step = 128
    for at in range(0, features, step):
        wg_v[at:at + step, :] = (
            wg_acc[at:at + step, :] + lax.dot_general(
                late_rows[:, at:at + step], late_hid[...], (((0,), (0,)), ((), ())),
                preferred_element_type=F32,
            )
        ).astype(BF16)
        write(wg_v, wg_out, pl.ds(at, step), 2)
    size = slots // 4
    for at in range(0, slots, size):
        for k, delta, staged, out in ((0, a_gate, gate_v, gate_out), (1, a_up, up_v, up_out)):
            factor = scales[4 * k:4 * k + 1, 0:1]

            @pl.loop(0, size // 32)
            def _(j):
                part = pl.ds(pl.multiple_of(at + j * 32, 32), 32)
                staged[part, :] = (delta[part, :] * factor).astype(BF16)

            write(staged, out, pl.ds(at, size), k)
    for k, out in enumerate((gate_out, up_out, wg_out, router_out)):
        landed(out, sem.at[k])


def shards(out_grad, router_probs, expert_ids, saved_gate, saved_up, down_weight):
    tok, top = expert_ids.shape
    experts = lax.axis_size("expert")
    cap = saved_gate.shape[3]
    width = saved_gate.shape[4]
    slots = saved_gate.shape[2] * cap
    features = down_weight.shape[1]
    half = slots // 2
    chips = experts // 2
    any_space = pl.BlockSpec(memory_space=pl.ANY)
    hbm = pl.BlockSpec(memory_space=pltpu.HBM)
    vmem = pl.BlockSpec(memory_space=pltpu.VMEM)
    dma = pltpu.SemaphoreType.DMA
    stay = functools.partial(pltpu.with_memory_space_constraint, memory_space=pltpu.HBM)
    shapes = (
        ((slots, width), BF16), ((slots, width), BF16), ((features, width), BF16),
        ((top, tok), F32),
    )
    last = half // 2
    between = (
        ((slots, width), F32), ((slots, width), F32), ((features, width), F32),
        ((last, features), BF16), ((last, width), BF16), ((8, 128), F32), ((top, tok), F32),
    )
    results = pl.pallas_call(
        functools.partial(kernel, experts, cap, tok, top),
        out_shape=tuple(pltpu.VMEM(*shape) for shape in between),
        in_specs=[hbm] * 6,
        out_specs=(vmem,) * len(between),
        scratch_shapes=[
            pltpu.VMEM((top, tok), jnp.int32),
            pltpu.VMEM((top, tok), BF16),
            pltpu.VMEM((2, tok, features // 2), BF16),
            pltpu.VMEM((slots, width), BF16),
            pltpu.VMEM((slots, width), BF16),
            pltpu.VMEM((features, width), BF16),
            pltpu.VMEM((RING, slots, width), BF16),
            pltpu.VMEM((RING, slots, features), BF16),
            pltpu.VMEM((2, tok, features // 2), BF16),
            pltpu.VMEM((8, 128), F32),
            pltpu.VMEM((2, 8, 128), F32),
            pltpu.VMEM((2 * cap * experts, features // 2), BF16),
            pltpu.VMEM((RING, 2, half, width), F32),
            pltpu.VMEM((RING, 2, half, width), BF16),
            pltpu.VMEM((2, half, width), BF16),
            pltpu.VMEM((2, half, width), BF16),
            pltpu.VMEM((2, half, width), BF16),
            pltpu.VMEM((2, half, width), BF16),
            pltpu.VMEM((8, 128), F32),
            pltpu.VMEM((RING, 8, 128), F32),
            pltpu.VMEM((8, 128), F32),
            pltpu.VMEM((RING, 8, 128), F32),
            pltpu.VMEM((slots + 128, 128), F32),
            pltpu.VMEM((1, slots + 128), F32),
            pltpu.VMEM((experts, 1, slots + 128), F32),
            pltpu.VMEM((experts, 128), F32),
            pltpu.VMEM((RING, experts, 128), F32),
            dma((10,)),
            dma((2,)), dma((2,)), dma((2,)), dma((2,)),
            dma((1,)), dma((chips,)),
            dma((1,)), dma((chips + 1,)),
            dma((1,)), dma((6,)),
            dma((1,)), dma((5,)),
            dma((1,)), dma((1,)), dma((1,)), dma((1,)),
            dma((1,)), dma((1,)),
            dma((1,)), dma((1,)),
        ],
        compiler_params=pltpu.CompilerParams(
            collective_id=0, has_side_effects=True, vmem_limit_bytes=40 * 1024 * 1024
        ),
        cost_estimate=pl.CostEstimate(
            flops=4 * RING * slots * features * width,
            bytes_accessed=4 * slots * width + 2 * features * width,
            transcendentals=slots * width,
        ),
    )(
        stay(out_grad), stay(expert_ids.T), stay(router_probs.T), stay(saved_gate.reshape(slots, width)),
        stay(saved_up.reshape(slots, width)), stay(down_weight.reshape(features, width)),
    )
    gate_grad, up_grad, weight_grad, router_grad = pl.pallas_call(
        finish,
        out_shape=tuple(jax.ShapeDtypeStruct(*shape) for shape in shapes),
        in_specs=[vmem] * len(between),
        out_specs=(any_space,) * 4,
        scratch_shapes=[pltpu.VMEM(*shape) for shape in shapes[:3]] + [dma((4,))],
        compiler_params=pltpu.CompilerParams(vmem_limit_bytes=8 * 1024 * 1024),
    )(*(pltpu.with_memory_space_constraint(r, memory_space=pltpu.VMEM) for r in results))
    return (
        gate_grad.reshape(saved_gate.shape), up_grad.reshape(saved_up.shape),
        weight_grad.reshape(down_weight.shape), router_grad.T,
    )


def solution(mesh):
    in_specs = (
        P(("expert", "edata"), None),
        P(("expert", "edata"), None),
        P(("expert", "edata"), None),
        P("expert", "edata", None, None, "tensor"),
        P("expert", "edata", None, None, "tensor"),
        P("expert", "edata", "tensor"),
    )
    out_specs = (
        P("expert", "edata", None, None, "tensor"),
        P("expert", "edata", None, None, "tensor"),
        P("expert", "edata", "tensor"),
        P(("expert", "edata"), None),
    )
    return jax.shard_map(shards, mesh=mesh, in_specs=in_specs, out_specs=out_specs, check_vma=False)
```

```python
import functools

import jax
import jax.numpy as jnp
from jax import lax
from jax.experimental import pallas as pl
from jax.experimental.pallas import tpu as pltpu
from jax.sharding import PartitionSpec as P

MESH = pl.DeviceIdType.MESH
RING = 4
F32 = jnp.float32
BF16 = jnp.bfloat16


def local(src, dst, sem):
    return pltpu.make_async_copy(src, dst, sem)


def landed(ref, sem):
    pltpu.make_async_copy(ref, ref, sem).wait()


def silu_factors(gate_value, up_value):
    sigmoid_gate = jax.nn.sigmoid(gate_value)
    activated = gate_value * sigmoid_gate
    gate_factor = up_value * sigmoid_gate * (1.0 + gate_value * (1.0 - sigmoid_gate))
    return activated * up_value, gate_factor, activated


def kernel(
    experts, cap, tok, top,
    og, ids, probs, gate, up, w,
    a_gate, a_up, wg_acc, late_rows, late_hid, scales, router_out,
    ids_ref, probs_ref, og_v, gate_v, up_v, w_v, hid, rows, x2, meta_own, meta_in, sb,
    part_f, part_b, sb_c, rb_o, rb_d, rb_c,
    pk_own, pk_in, pk_row, pk_rows, rl, rz_out, rz_in, ry_own, ry_in,
    load_sem, xs, xr, ms, mr, zs, zr, ys, yr, hs, hr, bs, br, ps, pr, qs, qr, ws, wr, vs, vr,
):
    e, x, y = lax.axis_index("expert"), lax.axis_index("edata"), lax.axis_index("tensor")
    z, c = lax.div(e, 2), lax.rem(e, 2)
    slots, width = gate.shape
    half = slots // 2
    quarter = half // 2
    features = w.shape[0]
    lanes_half = features // 2
    pair = 2 * cap
    x_right, x_left, x_far = lax.rem(x + 1, RING), lax.rem(x + 3, RING), lax.rem(x + 2, RING)
    y_right, y_left, y_far = lax.rem(y + 1, RING), lax.rem(y + 3, RING), lax.rem(y + 2, RING)
    first, second = pl.ds(0, half), pl.ds(half, half)
    fill_right = x == y
    fill_left = x == y

    def share(core):
        return lax.rem(y - x + 2 * core + RING, RING)

    from_y = lax.rem(x + y + 2 * c, RING)
    gives_home = jnp.logical_and(share(1 - c) == x, x == y)
    takes_home = jnp.logical_and(from_y == y, x == y)
    stays = jnp.logical_and(share(c) == x, x == y)
    gives_near = jnp.logical_or(share(c) == x, x == y)
    takes_near = jnp.logical_or(from_y == y, x == y)

    barrier = pltpu.get_barrier_semaphore()

    def greet(device):
        pl.semaphore_signal(barrier, inc=1, device_id=device, device_id_type=MESH)

    @pl.loop(1, experts)
    def _(i):
        greet((lax.rem(e + i, experts), x, y))

    for i in range(1, RING):
        greet((e, lax.rem(x + i, RING), y))
        greet((e, x, lax.rem(y + i, RING)))

    @pl.when(jnp.logical_not(gives_near))
    def _():
        greet((e, share(c), x))

    @pl.when(jnp.logical_not(takes_near))
    def _():
        greet((e, y, from_y))

    @pl.when(jnp.logical_not(gives_home))
    def _():
        greet((2 * z + 1 - c, share(1 - c), x))

    @pl.when(jnp.logical_not(takes_home))
    def _():
        greet((2 * z + 1 - c, y, from_y))

    loads = [
        tuple(
            local(ref.at[part], held.at[part], load_sem.at[6 + 2 * i + k])
            for k, (ref, held) in enumerate(((gate, gate_v), (up, up_v)))
        )
        for i, part in enumerate((first, second))
    ]
    load_w = local(w, w_v, load_sem.at[2])
    small = (
        local(ids, ids_ref, load_sem.at[3]),
        local(probs, probs_ref, load_sem.at[4]),
    )
    tokens = tuple(
        local(
            og.at[:, pl.ds(
                pl.multiple_of(features * share(core) + lanes_half * core, 128), lanes_half
            )],
            og_v.at[core], load_sem.at[5],
        )
        for core in range(2)
    )
    for copy in small + tokens:
        copy.start()
    for copy in loads[0] + loads[1]:
        copy.start()
    load_w.start()

    place = (
        lax.broadcasted_iota(jnp.int32, (tok, 128), 1)
        == lax.broadcasted_iota(jnp.int32, (tok, 128), 0) + tok * c
    ).astype(F32).astype(BF16)
    for copy in small:
        copy.wait()
    meta_own[0:top, :] = jnp.dot(
        ids_ref[...].astype(F32).astype(BF16), place, preferred_element_type=F32
    )
    meta_own[4:4 + top, :] = jnp.dot(probs_ref[...], place, preferred_element_type=F32)

    def hidden_of(i):
        for copy in loads[i]:
            copy.wait()

        @pl.loop(0, half // 32)
        def _(j):
            part = pl.ds(pl.multiple_of(i * half + j * 32, 32), 32)
            for at in range(0, width, 128):
                lanes = slice(at, at + 128)
                hidden, gate_factor, up_factor = silu_factors(
                    gate_v[part, lanes].astype(F32), up_v[part, lanes].astype(F32)
                )
                hid[x, part, lanes] = hidden.astype(BF16)
                a_gate[part, lanes] = gate_factor
                a_up[part, lanes] = up_factor

    landed(og_v, load_sem.at[5])
    hidden_of(0)
    peers = experts - 1 + 2 * (RING - 1)
    for near in (gives_near, takes_near, gives_home, takes_home):
        peers = peers + jnp.where(near, 0, 1)
    pl.semaphore_wait(barrier, peers)

    def swap(core):
        device = (2 * z + core, share(core), x)
        return (
            pltpu.make_async_remote_copy(
                src_ref=meta_own, dst_ref=meta_in.at[c], send_sem=ms.at[core],
                recv_sem=mr.at[c], device_id=device, device_id_type=MESH,
            ),
            pltpu.make_async_remote_copy(
                src_ref=og_v.at[core], dst_ref=x2.at[c], send_sem=xs.at[core],
                recv_sem=xr.at[c], device_id=device, device_id_type=MESH,
            ),
        )

    for core in range(2):
        at_home = jnp.logical_and(stays, c == core)

        @pl.when(at_home)
        def _():
            local(meta_own, meta_in.at[c], mr.at[c]).start()
            local(og_v.at[core], x2.at[c], xr.at[c]).start()

        @pl.when(jnp.logical_not(at_home))
        def _():
            for copy in swap(core):
                copy.start()

    part_a, part_e = pl.ds(0, quarter), pl.ds(quarter, quarter)
    last = quarter // 2
    more = quarter - last
    part_c, part_d = pl.ds(quarter, more), pl.ds(quarter + more, last)
    far_a = pl.ds(half, quarter)
    far_c, far_d = pl.ds(half + quarter, more), pl.ds(half + quarter + more, last)

    def pass_hidden(index, block, part, to_right):
        at = hid.at[block, part]
        return pltpu.make_async_remote_copy(
            src_ref=at, dst_ref=at, send_sem=hs.at[0], recv_sem=hr.at[index],
            device_id=(e, x_right if to_right else x_left, y), device_id_type=MESH,
        )

    h_r0 = pass_hidden(0, x, first, True)
    h_r1 = pass_hidden(2, x, second, True)
    h_l0 = pass_hidden(2, x, first, False)
    h_l1 = pass_hidden(1, x, second, False)
    h_ra = pass_hidden(3, x_left, part_a, True)
    h_la = pass_hidden(3, x_right, far_a, False)
    h_rc = pass_hidden(4, x_left, part_c, True)
    h_lc = pass_hidden(4, x_right, far_c, False)
    h_rd = pass_hidden(5, x_left, part_d, True)
    h_ld = pass_hidden(5, x_right, far_d, False)
    h_r0.start()
    hidden_of(1)
    for copy in (h_l1, h_r1, h_l0):
        copy.start()
    for core in range(2):
        local(meta_own, meta_in.at[core], mr.at[core]).wait()
        local(x2.at[core], x2.at[core], xr.at[core]).wait()
    meta = meta_in[0] + meta_in[1]
    lane = lax.broadcasted_iota(jnp.int32, (experts, 128), 1)
    expert_row = lax.broadcasted_iota(jnp.int32, (experts, 128), 0).astype(F32)
    member = jnp.zeros((experts, 128), F32)
    scale = jnp.zeros((experts, 128), F32)
    for k in range(top):
        named = meta[k:k + 1, :] == expert_row
        member = jnp.where(named, 1.0, member)
        scale = jnp.where(named, meta[4 + k:5 + k, :], scale)
    live = lane < 2 * tok
    member = jnp.where(live, member, 0.0)
    row_i = lax.broadcasted_iota(jnp.int32, (128, 128), 0)
    lane_i = lax.broadcasted_iota(jnp.int32, (128, 128), 1)
    before = jnp.logical_and(row_i < lane_i, jnp.logical_or(row_i >= tok, lane_i < tok))
    earlier = jnp.dot(
        member.astype(BF16), before.astype(F32).astype(BF16), preferred_element_type=F32
    )
    target = jnp.where(
        member > 0.0, earlier + jnp.where(lane >= tok, float(cap), 0.0), -1.0
    )
    slot_row = lax.broadcasted_iota(jnp.int32, (experts, pair, 128), 1).astype(F32)
    pick = jnp.where(slot_row == target[:, None, :], scale[:, None, :], 0.0).astype(BF16)
    sb[...] = jnp.dot(
        pick.reshape(experts * pair, 128)[:, :2 * tok], x2[...].reshape(2 * tok, lanes_half),
        preferred_element_type=F32,
    ).astype(BF16)
    my_rows = pl.ds(pl.multiple_of(pair * z, 16), pair)
    my_lanes = pl.ds(pl.multiple_of(lanes_half * c, 128), lanes_half)

    def dispatch(to):
        return pltpu.make_async_remote_copy(
            src_ref=sb.at[pl.ds(pl.multiple_of(pair * to, 16), pair)],
            dst_ref=rows.at[y, my_rows, my_lanes],
            send_sem=zs.at[0], recv_sem=zr.at[z],
            device_id=(to, x, y), device_id_type=MESH,
        )

    chips = experts // 2

    def chip(j):
        away = lax.div(j + 1, 2)
        return lax.rem(jnp.where(lax.rem(j, 2) == 1, z + away, z - away + chips), chips)

    local(
        sb.at[pl.ds(pl.multiple_of(pair * e, 16), pair)], rows.at[y, my_rows, my_lanes], zr.at[z]
    ).start()
    dispatch(2 * z + 1 - c).start()

    def dispatch_both(j):
        for core in range(2):
            dispatch(2 * chip(j) + core).start()

    @pl.loop(1, chips)
    def _(j):
        dispatch_both(j)

    def pass_rows(j, block, to_right, sem):
        at = rows.at[block, pl.ds(pl.multiple_of(pair * chip(j), 16), pair)]
        return pltpu.make_async_remote_copy(
            src_ref=at, dst_ref=at, send_sem=ys.at[0], recv_sem=yr.at[sem],
            device_id=(e, x, y_right if to_right else y_left), device_id_type=MESH,
        )

    def go_right(j):
        return pass_rows(j, y, True, j)

    def go_left(j):
        return pass_rows(j, y, False, j)

    def on_right(j):
        return pass_rows(j, y_left, True, chips)

    def on_left(j):
        return pass_rows(j, y_right, False, chips)

    def start_own(j):
        landed(
            rows.at[y, pl.ds(pl.multiple_of(pair * chip(j), 16), pair)], zr.at[chip(j)]
        )
        go_right(j).start()
        go_left(j).start()

    def start_on(j):
        landed(rows.at[pl.ds(0, 2), pl.ds(0, pair)], yr.at[j])

        (on_right, on_left)[j % 2](j).start()

    tiles = [(at, min(256, width - at)) for at in range(0, width, 256)]

    def send(index, src, dst, to_right):
        return pltpu.make_async_remote_copy(
            src_ref=src, dst_ref=dst, send_sem=bs.at[0], recv_sem=br.at[index],
            device_id=(e, x_right if to_right else x_left, y), device_id_type=MESH,
        )

    far0 = send(0, part_b.at[2, 0], rb_o.at[0], True)
    far1 = send(1, part_b.at[2, 1], rb_o.at[1], False)
    near0, near1 = (
        [
            send(2, part_b.at[role, 1 - k, part], rb_d.at[k, part], k == 0)
            for part in (part_a, part_e)
        ]
        for k, role in enumerate((1, 3))
    )
    both = [
        (send(3 + i, sb_c.at[0, part], rb_c.at[0, part], True),
         send(3 + i, sb_c.at[1, part], rb_c.at[1, part], False))
        for i, part in enumerate((part_a, part_e))
    ]

    def partial(replica):
        role = lax.rem(replica - x + RING, RING)
        block = rows[replica]
        for at, size in tiles:
            product = jnp.dot(block, w_v[:, at:at + size], preferred_element_type=F32)
            for i in range(2):
                value = product[i * half:(i + 1) * half]
                part_f[role, i, :, at:at + size] = value
                part_b[role, i, :, at:at + size] = value.astype(BF16)

        @pl.when(role == 2)
        def _():
            far0.start()
            far1.start()

        @pl.when(role == 1)
        def _():
            near0[0].start()

        @pl.when(role == 3)
        def _():
            near1[0].start()

    for j in range(chips):
        start_own(j)

    @pl.when(fill_right)
    def _():
        h_r0.wait_recv()
        h_rc.start()

    @pl.when(fill_left)
    def _():
        h_l1.wait_recv()
        h_lc.start()

    load_w.wait()
    partial(y)

    for k in range(chips):
        start_on(k)

    partial(jnp.where(x == y_right, y_left, y_right))
    partial(jnp.where(x == y_right, y_right, y_left))

    landed(rows.at[y_far], yr.at[chips])
    partial(y_far)
    near0[1].start()
    near1[1].start()

    @pl.when(jnp.logical_not(fill_right))
    def _():
        h_r0.wait_recv()

    @pl.when(jnp.logical_not(fill_left))
    def _():
        h_l1.wait_recv()

    landed(hid.at[x], hr.at[2])
    step = 256 if features % 256 == 0 else 128

    def outer(block, slot_parts, at):
        left = jnp.concatenate([rows[block, p, at:at + step] for p in slot_parts], axis=0)
        right = jnp.concatenate([hid[block, p, :] for p in slot_parts], axis=0)
        return lax.dot_general(
            left, right, (((0,), (0,)), ((), ())), preferred_element_type=F32
        )

    everything = (slice(0, slots),)
    for at in range(0, features, step):
        wg_acc[at:at + step, :] = (
            outer(x, everything, at) + outer(x_left, everything, at) + outer(x_right, everything, at)
        )
    early = (slice(0, quarter), slice(half, half + quarter))
    late = tuple(slice(at, at + more) for at in (quarter, half + quarter))
    latest = tuple(slice(at + more, at + quarter) for at in (quarter, half + quarter))

    for core in range(2):
        @pl.when(jnp.logical_not(jnp.logical_and(stays, c == core)))
        def _():
            for copy in swap(core):
                copy.wait_send()

    landed(sb.at[pl.ds(0, pair * (experts - 1))], zs.at[0])
    landed(rows.at[pl.ds(0, 3)], ys.at[0])

    def pass_on(side):
        @pl.when(side == 0)
        def _():
            far0.wait_recv()

        @pl.when(side == 1)
        def _():
            far1.wait_recv()

        for i in range(2):
            @pl.loop(0, quarter // 16)
            def _(j):
                part = pl.ds(pl.multiple_of(i * quarter + j * 16, 16), 16)
                sb_c[side, part, :] = (
                    part_f[1 + 2 * side, side, part, :] + rb_o[side, part, :].astype(F32)
                ).astype(BF16)

            for k in range(2):
                @pl.when(side == k)
                def _():
                    both[i][k].start()

    early_side = jnp.where(x_left == y, 1, 0)
    pass_on(early_side)
    pass_on(1 - early_side)

    h_ra.start()
    h_la.start()

    landed(rb_d, br.at[2])

    zero = jnp.zeros((16, 128), F32)
    peaks = (zero, zero)
    for i in range(2):
        landed(rb_c.at[pl.ds(0, 2), pl.ds(0, quarter)], br.at[3 + i])
        for side in range(2):
            def body(j, carry):
                gate_peak, up_peak = carry
                part = pl.ds(pl.multiple_of(i * quarter + j * 16, 16), 16)
                at = pl.ds(pl.multiple_of(side * half + i * quarter + j * 16, 16), 16)
                sent = rb_d[1 - side, part, :].astype(F32) + rb_c[side, part, :].astype(F32)
                d_hidden = part_f[0, side, part, :] + sent
                gate_delta = d_hidden * a_gate[at, :]
                up_delta = d_hidden * a_up[at, :]
                a_gate[at, :] = gate_delta
                a_up[at, :] = up_delta
                weighted = up_delta * up_v[at, :].astype(F32)
                total = zero
                for lane0 in range(0, width, 128):
                    sl = slice(lane0, lane0 + 128)
                    gate_peak = jnp.maximum(gate_peak, jnp.abs(gate_delta[:, sl]))
                    up_peak = jnp.maximum(up_peak, jnp.abs(up_delta[:, sl]))
                    total = total + weighted[:, sl]
                rl[at, :] = total
                return gate_peak, up_peak

            peaks = lax.fori_loop(0, quarter // 16, body, peaks)
    peak_row = lax.broadcasted_iota(jnp.int32, (8, 128), 0)
    pk_own[...] = jnp.where(
        peak_row < 4,
        jnp.max(peaks[0], axis=0, keepdims=True), jnp.max(peaks[1], axis=0, keepdims=True),
    )

    def tell_row(p):
        return pltpu.make_async_remote_copy(
            src_ref=pk_own, dst_ref=pk_in.at[y], send_sem=ps.at[0], recv_sem=pr.at[0],
            device_id=(e, x, p), device_id_type=MESH,
        )

    def tell_column(p):
        return pltpu.make_async_remote_copy(
            src_ref=pk_row, dst_ref=pk_rows.at[x], send_sem=qs.at[0], recv_sem=qr.at[0],
            device_id=(e, p, y), device_id_type=MESH,
        )

    y_others, x_others = (y_right, y_left, y_far), (x_right, x_left, x_far)
    for p in y_others:
        tell_row(p).start()

    rl[slots:, :] = jnp.zeros((rl.shape[0] - slots, 128), F32)
    ones = jnp.ones((8, 128), BF16)
    across = (((1,), (1,)), ((), ()))

    def split(value):
        high = value.astype(BF16)
        return high, (value - high.astype(F32)).astype(BF16)

    sums = sum(
        lax.dot_general(ones, part, across, preferred_element_type=F32) for part in split(rl[...])
    )
    rz_out[...] = sums[0:1, :]

    def give_back(to):
        return pltpu.make_async_remote_copy(
            src_ref=rz_out, dst_ref=rz_in.at[e], send_sem=ws.at[0], recv_sem=wr.at[0],
            device_id=(to, x, y), device_id_type=MESH,
        )

    @pl.loop(1, experts)
    def _(i):
        give_back(lax.rem(e + i, experts)).start()

    rz_in[e] = rz_out[...]
    row_peak = pk_own[...]
    landed(pk_in.at[pl.ds(0, 3)], pr.at[0])
    for p in y_others:
        row_peak = jnp.maximum(row_peak, pk_in[p])
    pk_row[...] = row_peak
    for p in x_others:
        tell_column(p).start()

    @pl.when(jnp.logical_not(fill_right))
    def _():
        h_rc.start()

    @pl.when(jnp.logical_not(fill_left))
    def _():
        h_lc.start()

    h_rd.start()
    h_ld.start()
    landed(rz_in.at[pl.ds(0, experts - 1)], wr.at[0])
    from_experts = rz_in[:, 0, :]
    mine = (
        lax.broadcasted_iota(jnp.int32, (128, from_experts.shape[1]), 1)
        == lax.broadcasted_iota(jnp.int32, (128, from_experts.shape[1]), 0) + cap * e
    ).astype(F32).astype(BF16)
    ry_own[...] = sum(
        lax.dot_general(part, mine, across, preferred_element_type=F32)
        for part in split(from_experts)
    )

    def tell_sum(p):
        return pltpu.make_async_remote_copy(
            src_ref=ry_own, dst_ref=ry_in.at[y], send_sem=vs.at[0], recv_sem=vr.at[0],
            device_id=(e, x, p), device_id_type=MESH,
        )

    for p in y_others:
        tell_sum(p).start()

    landed(hid.at[x_far, pl.ds(0, 2 * quarter)], hr.at[3])
    for at in range(0, features, step):
        wg_acc[at:at + step, :] += outer(x_far, early, at)

    all_peaks = row_peak
    landed(pk_rows.at[pl.ds(0, 3)], qr.at[0])
    for p in x_others:
        all_peaks = jnp.maximum(all_peaks, pk_rows[p])
    scales[...] = 1.0 / (
        jnp.where(
            peak_row < 4,
            jnp.max(all_peaks[:4], axis=(0, 1), keepdims=True),
            jnp.max(all_peaks[4:], axis=(0, 1), keepdims=True),
        ) + 1e-6
    )
    landed(hid.at[x_far, pl.ds(0, 2 * more)], hr.at[4])
    for at in range(0, features, step):
        wg_acc[at:at + step, :] += outer(x_far, late, at)

    ids_f = ids_ref[...].astype(F32)
    expert_col = lax.broadcasted_iota(jnp.int32, (experts, tok), 0).astype(F32)
    named = [(ids_f[k:k + 1, :] == expert_col).astype(F32) for k in range(top)]
    tri = (
        lax.broadcasted_iota(jnp.int32, (tok, tok), 0)
        < lax.broadcasted_iota(jnp.int32, (tok, tok), 1)
    ).astype(F32).astype(BF16)
    earlier = jnp.dot(sum(named).astype(BF16), tri, preferred_element_type=F32)
    slot_col = lax.broadcasted_iota(jnp.int32, (128, tok), 0).astype(F32)
    at_slot = [
        slot_col == jnp.sum(earlier * named[k], axis=0, keepdims=True) for k in range(top)
    ]
    landed(ry_in.at[pl.ds(0, 3)], vr.at[0])
    sums = ry_own[...]
    for p in y_others:
        sums = sums + ry_in[p]
    high, low = split(sums)
    down = (((0,), (0,)), ((), ()))
    for k in range(top):
        pick = named[k].astype(BF16)
        found = lax.dot_general(
            high, pick, down, preferred_element_type=F32
        ) + lax.dot_general(low, pick, down, preferred_element_type=F32)
        value = jnp.sum(jnp.where(at_slot[k], found, 0.0), axis=0, keepdims=True)
        router_out[k:k + 1, :] = value / probs_ref[k:k + 1, :].astype(F32)

    landed(hid.at[x_far, pl.ds(0, 2 * last)], hr.at[5])
    late_rows[...] = jnp.concatenate([rows[x_far, p, :] for p in latest], axis=0)
    late_hid[...] = jnp.concatenate([hid[x_far, p, :] for p in latest], axis=0)

    landed(rz_in.at[pl.ds(0, experts - 1)], ws.at[0])
    landed(ry_in.at[pl.ds(0, 3)], vs.at[0])
    landed(pk_in.at[pl.ds(0, 3)], ps.at[0])
    landed(pk_rows.at[pl.ds(0, 3)], qs.at[0])
    landed(hid.at[pl.ds(0, 3)], hs.at[0])
    landed(part_b.at[pl.ds(0, 3)], bs.at[0])


def finish(
    a_gate, a_up, wg_acc, late_rows, late_hid, scales, router, gate_out, up_out, wg_out, router_out,
    gate_v, up_v, wg_v, sem,
):
    local(router, router_out, sem.at[3]).start()

    def write(source, target, part, k):
        local(source.at[part], target.at[part], sem.at[k]).start()

    slots, features = a_gate.shape[0], wg_acc.shape[0]
    step = 128
    for at in range(0, features, step):
        wg_v[at:at + step, :] = (
            wg_acc[at:at + step, :] + lax.dot_general(
                late_rows[:, at:at + step], late_hid[...], (((0,), (0,)), ((), ())),
                preferred_element_type=F32,
            )
        ).astype(BF16)
        write(wg_v, wg_out, pl.ds(at, step), 2)
    size = slots // 4
    for at in range(0, slots, size):
        for k, delta, staged, out in ((0, a_gate, gate_v, gate_out), (1, a_up, up_v, up_out)):
            factor = scales[4 * k:4 * k + 1, 0:1]

            @pl.loop(0, size // 32)
            def _(j):
                part = pl.ds(pl.multiple_of(at + j * 32, 32), 32)
                staged[part, :] = (delta[part, :] * factor).astype(BF16)

            write(staged, out, pl.ds(at, size), k)
    for k, out in enumerate((gate_out, up_out, wg_out, router_out)):
        landed(out, sem.at[k])


def shards(out_grad, router_probs, expert_ids, saved_gate, saved_up, down_weight):
    tok, top = expert_ids.shape
    experts = lax.axis_size("expert")
    cap = saved_gate.shape[3]
    width = saved_gate.shape[4]
    slots = saved_gate.shape[2] * cap
    features = down_weight.shape[1]
    half = slots // 2
    chips = experts // 2
    any_space = pl.BlockSpec(memory_space=pl.ANY)
    hbm = pl.BlockSpec(memory_space=pltpu.HBM)
    vmem = pl.BlockSpec(memory_space=pltpu.VMEM)
    dma = pltpu.SemaphoreType.DMA
    stay = functools.partial(pltpu.with_memory_space_constraint, memory_space=pltpu.HBM)
    shapes = (
        ((slots, width), BF16), ((slots, width), BF16), ((features, width), BF16),
        ((top, tok), F32),
    )
    last = half // 2
    between = (
        ((slots, width), F32), ((slots, width), F32), ((features, width), F32),
        ((last, features), BF16), ((last, width), BF16), ((8, 128), F32), ((top, tok), F32),
    )
    results = pl.pallas_call(
        functools.partial(kernel, experts, cap, tok, top),
        out_shape=tuple(pltpu.VMEM(*shape) for shape in between),
        in_specs=[hbm] * 6,
        out_specs=(vmem,) * len(between),
        scratch_shapes=[
            pltpu.VMEM((top, tok), jnp.int32),
            pltpu.VMEM((top, tok), BF16),
            pltpu.VMEM((2, tok, features // 2), BF16),
            pltpu.VMEM((slots, width), BF16),
            pltpu.VMEM((slots, width), BF16),
            pltpu.VMEM((features, width), BF16),
            pltpu.VMEM((RING, slots, width), BF16),
            pltpu.VMEM((RING, slots, features), BF16),
            pltpu.VMEM((2, tok, features // 2), BF16),
            pltpu.VMEM((8, 128), F32),
            pltpu.VMEM((2, 8, 128), F32),
            pltpu.VMEM((2 * cap * experts, features // 2), BF16),
            pltpu.VMEM((RING, 2, half, width), F32),
            pltpu.VMEM((RING, 2, half, width), BF16),
            pltpu.VMEM((2, half, width), BF16),
            pltpu.VMEM((2, half, width), BF16),
            pltpu.VMEM((2, half, width), BF16),
            pltpu.VMEM((2, half, width), BF16),
            pltpu.VMEM((8, 128), F32),
            pltpu.VMEM((RING, 8, 128), F32),
            pltpu.VMEM((8, 128), F32),
            pltpu.VMEM((RING, 8, 128), F32),
            pltpu.VMEM((slots + 128, 128), F32),
            pltpu.VMEM((1, slots + 128), F32),
            pltpu.VMEM((experts, 1, slots + 128), F32),
            pltpu.VMEM((experts, 128), F32),
            pltpu.VMEM((RING, experts, 128), F32),
            dma((10,)),
            dma((2,)), dma((2,)), dma((2,)), dma((2,)),
            dma((1,)), dma((chips,)),
            dma((1,)), dma((chips + 1,)),
            dma((1,)), dma((6,)),
            dma((1,)), dma((5,)),
            dma((1,)), dma((1,)), dma((1,)), dma((1,)),
            dma((1,)), dma((1,)),
            dma((1,)), dma((1,)),
        ],
        compiler_params=pltpu.CompilerParams(
            collective_id=0, has_side_effects=True, vmem_limit_bytes=40 * 1024 * 1024
        ),
        cost_estimate=pl.CostEstimate(
            flops=4 * RING * slots * features * width,
            bytes_accessed=4 * slots * width + 2 * features * width,
            transcendentals=slots * width,
        ),
    )(
        stay(out_grad), stay(expert_ids.T), stay(router_probs.T), stay(saved_gate.reshape(slots, width)),
        stay(saved_up.reshape(slots, width)), stay(down_weight.reshape(features, width)),
    )
    gate_grad, up_grad, weight_grad, router_grad = pl.pallas_call(
        finish,
        out_shape=tuple(jax.ShapeDtypeStruct(*shape) for shape in shapes),
        in_specs=[vmem] * len(between),
        out_specs=(any_space,) * 4,
        scratch_shapes=[pltpu.VMEM(*shape) for shape in shapes[:3]] + [dma((4,))],
        compiler_params=pltpu.CompilerParams(vmem_limit_bytes=8 * 1024 * 1024),
    )(*(pltpu.with_memory_space_constraint(r, memory_space=pltpu.VMEM) for r in results))
    return (
        gate_grad.reshape(saved_gate.shape), up_grad.reshape(saved_up.shape),
        weight_grad.reshape(down_weight.shape), router_grad.T,
    )


def solution(mesh):
    in_specs = (
        P(("expert", "edata"), None),
        P(("expert", "edata"), None),
        P(("expert", "edata"), None),
        P("expert", "edata", None, None, "tensor"),
        P("expert", "edata", None, None, "tensor"),
        P("expert", "edata", "tensor"),
    )
    out_specs = (
        P("expert", "edata", None, None, "tensor"),
        P("expert", "edata", None, None, "tensor"),
        P("expert", "edata", "tensor"),
        P(("expert", "edata"), None),
    )
    return jax.shard_map(shards, mesh=mesh, in_specs=in_specs, out_specs=out_specs, check_vma=False)
```
